32 devices in a mesh: rep: 4 (over y, x), row: 2 (over core), col: 4 (over z).
Axes of the slice: x: 2, y: 2, z: 4, core: 2. Of those that a mesh axis runs over, the one named last changes fastest.
Arguments:
- tokens: bfloat16 [6144, 4096], P('rep', 'row'), may hold values from -6 to 6
- cotangent: bfloat16 [6144, 512], P(('rep', 'row'), 'col'), may hold values from -4 to 4
- weight: float32 [4, 4096, 512], P('rep', 'row', 'col'), may hold values from -0.09375 to 0.09375
- first_moment: float32 [4, 4096, 512], P('rep', 'row', 'col'), may hold values from -6 to 6
- second_moment: float32 [4, 4096, 512], P('rep', 'row', 'col'), may hold values from 1 to 10
- outer_delta: float32 [4, 1310720], P('rep', ('row', 'col')), may hold values from -6 to 6
- global_params: float32 [2, 1310720], P(None, ('row', 'col')), may hold values from -6 to 6
- outer_moment: float32 [2, 1310720], P(None, ('row', 'col')), may hold values from -6 to 6
- group_slot: int32 [1], replicated, may hold values from 0 to 1
Outputs:
- keys_values: bfloat16 [6144, 512], P(('rep', 'row'), 'col')
- input_grad: bfloat16 [6144, 4096], P(('rep', 'col'), 'row')
- new_weight: float32 [4, 4096, 512], P('rep', 'row', 'col')
- new_first: float32 [4, 4096, 512], P('rep', 'row', 'col')
- new_second: float32 [4, 4096, 512], P('rep', 'row', 'col')
- new_global: float32 [1310720], P(('row', 'col'))
- new_outer: float32 [1310720], P(('row', 'col'))
The draws below stay inside these ranges and needn't reach their ends.
Inputs may be any that keep to these rules, and one draw needn't show every extreme that they name: `group_slot`: the held group that the outer delta belongs to.
All inputs are finite; a program needn't handle non-finite values.
Results may differ from the reference program's by a relative error of at most 0.015.
Values may be sent and summed in bfloat16 or wider, within the bound.
No kernel may reach another device: no remote copies, remote signals or barrier semaphores. Data moves between devices by JAX's collectives and lax.ppermute only.
A program may use at most 64 MiB of HBM per device.

```python
import math
import jax
import jax.numpy as jnp
from jax import lax

DIN = 4096
HD = 128
KVC = 512
TOK = 1536
SLOTS = 2
GROUP = 1310720
N_REP = 4
N_COL = 4


def block_scale(rng, shape, shards, low, largest):
    level = 1.0
    for axis_at, shards_of in shards:
        draws = jax.random.uniform(jax.random.fold_in(jax.random.fold_in(rng, 6), axis_at), (shards_of,), jnp.float32, low / len(shards), largest / len(shards))
        level = level * jnp.repeat(jnp.exp(draws), shape[axis_at] // shards_of).reshape((-1,) + (1,) * (len(shape) - 1 - axis_at))
    return level


def bell_draw(own_key, shape, scale, bound, cuts=(), dtype=jnp.bfloat16):
    values = scale * jax.random.normal(own_key, shape, jnp.float32)
    if cuts:
        values = values * block_scale(own_key, shape, cuts, -0.22, 0.18)
    return jnp.clip(values, -bound, bound).astype(dtype)


def setup_inputs(seed: int = 0) -> dict:
    seeds = jax.random.split(jax.random.key(seed), 10)
    return {
        "tokens": bell_draw(seeds[0], (N_REP * TOK, DIN), 1.0, 6.0, ((0, 4), (1, 2))),
        "cotangent": bell_draw(seeds[1], (N_REP * TOK, KVC), 0.5, 4.0, ((0, 8), (1, 4))),
        "weight": bell_draw(seeds[2], (N_REP, DIN, KVC), DIN ** -0.5, 0.09375, ((0, 4), (1, 2), (2, 4)), jnp.float32),
        "first_moment": bell_draw(seeds[3], (N_REP, DIN, KVC), 1.0, 6.0, ((0, 4), (1, 2), (2, 4)), jnp.float32),
        "second_moment": jnp.clip(jnp.exp(math.log(10.0) - 2.3025851 * jax.random.uniform(seeds[4], (N_REP, DIN, KVC), jnp.float32) ** block_scale(seeds[4], (N_REP, DIN, KVC), ((0, 4), (1, 2), (2, 4)), -0.2, 0.2)), 1.0, 10.0),
        "outer_delta": bell_draw(seeds[5], (N_REP, GROUP), 1.0, 6.0, ((0, 4), (1, 8)), jnp.float32),
        "global_params": bell_draw(seeds[6], (SLOTS, GROUP), 1.0, 6.0, ((1, 8),), jnp.float32),
        "outer_moment": bell_draw(seeds[7], (SLOTS, GROUP), 1.0, 6.0, ((1, 8),), jnp.float32),
        "group_slot": jax.random.randint(seeds[8], (1,), 0, SLOTS).astype(jnp.int32),
    }


BETA_ONE = 0.9
BETA_TWO = 0.95
INNER_RATE = 0.0003
WEIGHT_DECAY = 0.1
EPSILON = 1e-08
OUTER_RATE = 0.7
NESTEROV = 0.9

def reference(tokens, cotangent, weight, first_moment, second_moment, outer_delta, global_params, outer_moment, group_slot):
    kv_list = []
    dx_list = []
    w_list = []
    m_list = []
    v_list = []
    for replica in range(N_REP):
        row_block = tokens[replica * TOK:(replica + 1) * TOK]
        cot_block = cotangent[replica * TOK:(replica + 1) * TOK]
        weight_bf = weight[replica].astype(jnp.bfloat16)
        kv_list.append(jnp.dot(row_block, weight_bf, preferred_element_type=jnp.float32).astype(jnp.bfloat16))
        gradient = jnp.dot(row_block.T, cot_block, preferred_element_type=jnp.float32)
        total = jnp.zeros((TOK, row_block.shape[1]), jnp.float32)
        for column in range(N_COL):
            piece = jnp.dot(cot_block[:, column * HD:(column + 1) * HD], weight_bf[:, column * HD:(column + 1) * HD].T, preferred_element_type=jnp.float32)
            total = total + lax.optimization_barrier(piece.astype(jnp.bfloat16)).astype(jnp.float32)
        dx_list.append(total.astype(jnp.bfloat16))
        first_new = BETA_ONE * first_moment[replica] + (1.0 - BETA_ONE) * gradient
        second_new = BETA_TWO * second_moment[replica] + (1.0 - BETA_TWO) * gradient * gradient
        w_list.append(weight[replica] - INNER_RATE * (first_new / (jnp.sqrt(second_new) + EPSILON) + WEIGHT_DECAY * weight[replica]))
        m_list.append(first_new)
        v_list.append(second_new)
    average = lax.optimization_barrier(jnp.sum(outer_delta, axis=0)) / N_REP
    chosen = group_slot[0].astype(jnp.int32)
    held_group = lax.dynamic_index_in_dim(global_params, chosen, 0, keepdims=False)
    prior_moment = lax.dynamic_index_in_dim(outer_moment, chosen, 0, keepdims=False)
    new_outer = NESTEROV * prior_moment + average
    new_global = held_group - OUTER_RATE * (average + NESTEROV * new_outer)
    return (jnp.concatenate(kv_list, axis=0), jnp.concatenate(dx_list, axis=0), jnp.stack(w_list), jnp.stack(m_list), jnp.stack(v_list), new_global, new_outer)
```

```python
import jax
import jax.numpy as jnp
from jax import lax
from jax.sharding import PartitionSpec as P

BETA_ONE = 0.9
BETA_TWO = 0.95
INNER_RATE = 0.0003
WEIGHT_DECAY = 0.1
EPSILON = 1e-08
OUTER_RATE = 0.7
NESTEROV = 0.9


def is_power_of_two(n):
    return n & (n - 1) == 0


def swap_pairs(n, bit):
    return [(i, i ^ bit) for i in range(n)]


def gather_offsets(block, axis):
    n = lax.axis_size(axis)
    have = {0: block}
    if is_power_of_two(n):
        bit = n // 2
        while bit:
            for k in list(have):
                have[k ^ bit] = lax.ppermute(have[k], axis, swap_pairs(n, bit))
            bit //= 2
        owner = lambda k: lax.axis_index(axis) ^ k
    else:
        for k in range(1, n):
            have[k] = lax.ppermute(have[k - 1], axis, [((i + 1) % n, i) for i in range(n)])
        owner = lambda k: (lax.axis_index(axis) + k) % n
    return have, owner


def row_gather(block, axis):
    n = lax.axis_size(axis)
    me = lax.axis_index(axis)
    parts = {0: block}
    for k in range(1, n):
        parts[k] = lax.ppermute(block, axis, [((i + k) % n, i) for i in range(n)])
    stacked = jnp.stack([parts[k] for k in range(n)])
    if n == 2:
        return jnp.where(me == 0, stacked, stacked[::-1])
    return jnp.roll(stacked, me, axis=0)


def my_cotangent(cotangent, rows, cols):
    per_row = cols // rows
    chunks = cotangent.reshape(per_row, cotangent.shape[0] // per_row, cotangent.shape[1])
    col = lax.axis_index("col")
    got = []
    for k in range(per_row):
        pairs = []
        for r in range(rows):
            for c in range(cols):
                pairs.append((r * cols + c, (c // per_row) * cols + r * per_row + (c + k) % per_row))
        send = lax.dynamic_index_in_dim(chunks, (col + k) % per_row, 0, keepdims=False)
        got.append(lax.ppermute(send, ("row", "col"), pairs))
    stacked = jnp.stack(got)
    ordered = jnp.take(stacked, (col - jnp.arange(per_row)) % per_row, axis=0)
    every = row_gather(ordered, "row")
    return every.reshape((cols,) + every.shape[2:])


def rep_sum(x, axis):
    n = lax.axis_size(axis)
    if not is_power_of_two(n):
        return lax.psum(x.astype(jnp.bfloat16), axis).astype(jnp.float32)
    bit = 1
    while bit < n:
        low = x.astype(jnp.bfloat16)
        x = low.astype(jnp.float32) + lax.ppermute(low, axis, swap_pairs(n, bit)).astype(jnp.float32)
        bit *= 2
    return x


def nesterov_merge(average, held_group, prior_moment):
    new_outer = NESTEROV * prior_moment + average
    new_global = held_group - OUTER_RATE * (average + NESTEROV * new_outer)
    return (new_global, new_outer)


def outer_step(outer_delta, global_params, outer_moment, group_slot):
    chosen = group_slot[0]
    held_group = lax.dynamic_index_in_dim(global_params, chosen, 0, keepdims=False)
    prior_moment = lax.dynamic_index_in_dim(outer_moment, chosen, 0, keepdims=False)
    replicas = lax.axis_size("rep")
    size = outer_delta.shape[1]
    average = rep_sum(outer_delta.reshape(size // 128, 128), "rep").reshape(size) / replicas
    return nesterov_merge(average, held_group, prior_moment)


def inner_step(tokens, cotangent, weight, first_moment, second_moment):
    rows, cols = lax.axis_size("row"), lax.axis_size("col")
    row = lax.axis_index("row")
    weight_bf = weight[0].astype(jnp.bfloat16)
    cot_mine = my_cotangent(cotangent, rows, cols)
    weights, owner = gather_offsets(weight_bf, "col")

    cot_full = row_gather(cotangent, "row").reshape(-1, cotangent.shape[1])
    partial = jnp.dot(tokens, weight_bf, preferred_element_type=jnp.float32)
    partial = partial.reshape(rows, partial.shape[0] // rows, partial.shape[1])
    keys_values = lax.dynamic_index_in_dim(partial, row, 0, keepdims=False)
    for k in range(1, rows):
        send = lax.dynamic_index_in_dim(partial, (row + k) % rows, 0, keepdims=False).astype(jnp.bfloat16)
        keys_values += lax.ppermute(send, "row", [(i, (i + k) % rows) for i in range(rows)]).astype(jnp.float32)
    keys_values = keys_values.astype(jnp.bfloat16)

    gradient = jnp.einsum("td,tc->dc", tokens, cot_full, preferred_element_type=jnp.float32)
    first_new = BETA_ONE * first_moment[0] + (1.0 - BETA_ONE) * gradient
    second_new = BETA_TWO * second_moment[0] + (1.0 - BETA_TWO) * gradient * gradient
    weight_new = weight[0] - INNER_RATE * (
        first_new / (jnp.sqrt(second_new) + EPSILON) + WEIGHT_DECAY * weight[0]
    )

    total = jnp.zeros((cot_mine.shape[1], weight_bf.shape[0]), jnp.float32)
    for k, block in weights.items():
        cot = lax.dynamic_index_in_dim(cot_mine, owner(k), 0, keepdims=False)
        total += jnp.einsum("th,dh->td", cot, block, preferred_element_type=jnp.float32)
    input_grad = total.astype(jnp.bfloat16)
    return (keys_values, input_grad, weight_new[None], first_new[None], second_new[None])


def on_device(
    tokens,
    cotangent,
    weight,
    first_moment,
    second_moment,
    outer_delta,
    global_params,
    outer_moment,
    group_slot,
):
    keys_values, input_grad, new_weight, new_first, new_second = inner_step(
        tokens, cotangent, weight, first_moment, second_moment
    )
    new_global, new_outer = outer_step(outer_delta, global_params, outer_moment, group_slot)
    return (keys_values, input_grad, new_weight, new_first, new_second, new_global, new_outer)


def solution(mesh):
    in_specs = (
        P("rep", "row"),
        P(("rep", "row"), "col"),
        P("rep", "row", "col"),
        P("rep", "row", "col"),
        P("rep", "row", "col"),
        P("rep", ("row", "col")),
        P(None, ("row", "col")),
        P(None, ("row", "col")),
        P(),
    )
    out_specs = (
        P(("rep", "row"), "col"),
        P(("rep", "col"), "row"),
        P("rep", "row", "col"),
        P("rep", "row", "col"),
        P("rep", "row", "col"),
        P(("row", "col")),
        P(("row", "col")),
    )
    return jax.shard_map(
        on_device, mesh=mesh, in_specs=in_specs, out_specs=out_specs, check_vma=False
    )
```

```python
import functools

import jax
import jax.numpy as jnp
from jax import lax
from jax.experimental import pallas as pl
from jax.experimental.pallas import tpu as pltpu
from jax.sharding import PartitionSpec as P

BETA_ONE = 0.9
BETA_TWO = 0.95
INNER_RATE = 0.0003
WEIGHT_DECAY = 0.1
EPSILON = 1e-08
OUTER_RATE = 0.7
NESTEROV = 0.9
LANES = 128
HALVES = 2

WHOLE = pl.BlockSpec(memory_space=pltpu.VMEM)
HBM = pl.BlockSpec(memory_space=pltpu.HBM)


def params(mebibytes):
    return pltpu.CompilerParams(vmem_limit_bytes=mebibytes * 1024 * 1024)


def after(x, others):
    return lax.optimization_barrier((x, others))


def in_hbm(x):
    return pltpu.with_memory_space_constraint(x, pltpu.HBM)


def is_power_of_two(n):
    return n & (n - 1) == 0


def swap_pairs(n, bit):
    return [(i, i ^ bit) for i in range(n)]


def shift_pairs(n, k):
    return [(i, (i + k) % n) for i in range(n)]


def mod(value, n):
    return lax.rem(value + n, n)


def gather_halves(halves, whole, axis):
    n = lax.axis_size(axis)
    have = [{0: (whole, h)} for h in range(len(halves))]
    if is_power_of_two(n):
        bit = n // 2
        for h, half in enumerate(halves):
            if bit > 1:
                have[h][bit] = (lax.ppermute(half, axis, swap_pairs(n, bit)), 0)
        while bit > 1:
            bit //= 2
            mine = lax.ppermute(whole, axis, swap_pairs(n, bit))
            for h in range(len(halves)):
                for k in list(have[h]):
                    have[h][k ^ bit] = (mine, h) if k == 0 else (lax.ppermute(have[h][k][0], axis, swap_pairs(n, bit)), 0)
        if n == 2:
            mine = lax.ppermute(whole, axis, swap_pairs(n, 1))
            for h in range(len(halves)):
                have[h][1] = (mine, h)
    else:
        moving = whole
        for k in range(1, n):
            moving = lax.ppermute(moving, axis, shift_pairs(n, n - 1))
            for h in range(len(halves)):
                have[h][k] = (moving, h)
    return [[have[h][k] for k in range(n)] for h in range(len(halves))]


def owner_of(me, k, n):
    return me ^ k if is_power_of_two(n) else mod(me + k, n)


def shifted(block, axis):
    n = lax.axis_size(axis)
    return [block] + [lax.ppermute(block, axis, shift_pairs(n, k)) for k in range(1, n)]


def chunk_pairs(rows, cols, per_row, k):
    pairs = []
    for r in range(rows):
        for c in range(cols):
            pairs.append((r * cols + c, (c // per_row) * cols + r * per_row + (c + k) % per_row))
    return pairs


def prepare_kernel(per_row, halves, weight_hbm, cot_hbm, delta_hbm, *refs):
    half_refs, whole_ref, low_ref = refs[:halves], refs[halves], refs[halves + 1]
    chunk_refs = refs[halves + 2:halves + 2 + per_row]
    weight_ref, delta_ref, weight_sems, chunk_sems, delta_sem = refs[-5:]
    depth = weight_ref.shape[0] // halves
    size = chunk_refs[0].shape[0]
    col = lax.axis_index("col")
    loads, chunks = [], []
    for h in range(halves):
        part = pl.ds(h * depth, depth)
        loads.append(pltpu.make_async_copy(weight_hbm.at[part, :], weight_ref.at[part, :], weight_sems.at[h]))
    for k in range(per_row):
        start = pl.multiple_of(lax.rem(col + k, per_row) * size, size)
        chunks.append(pltpu.make_async_copy(cot_hbm.at[pl.ds(start, size), :], chunk_refs[k], chunk_sems.at[k]))
    delta_load = pltpu.make_async_copy(delta_hbm, delta_ref, delta_sem)
    for copy in loads + chunks + [delta_load]:
        copy.start()
    for h in range(halves):
        loads[h].wait()
        part = pl.ds(h * depth, depth)
        low = weight_ref[part, :].astype(jnp.bfloat16)
        half_refs[h][...] = low
        whole_ref[part, :] = low
    delta_load.wait()
    low_ref[...] = delta_ref[...].astype(jnp.bfloat16)
    for copy in chunks:
        copy.wait()


def prepare(weight, cotangent, delta, per_row, halves):
    depth, width = weight.shape
    chunk = cotangent.shape[0] // per_row
    shape = lambda *s: jax.ShapeDtypeStruct(s, jnp.bfloat16)
    outs = [shape(depth // halves, width)] * halves + [shape(depth, width), shape(*delta.shape)] + [shape(chunk, width)] * per_row
    got = pl.pallas_call(
        functools.partial(prepare_kernel, per_row, halves),
        out_shape=outs,
        in_specs=[HBM] * 3,
        out_specs=[WHOLE] * len(outs),
        scratch_shapes=[
            pltpu.VMEM((depth, width), jnp.float32),
            pltpu.VMEM(delta.shape, jnp.float32),
            pltpu.SemaphoreType.DMA((halves,)),
            pltpu.SemaphoreType.DMA((per_row,)),
            pltpu.SemaphoreType.DMA,
        ],
        compiler_params=params(16),
        cost_estimate=pl.CostEstimate(flops=0, bytes_accessed=8 * weight.size, transcendentals=0),
        name="prepare",
    )(in_hbm(weight), in_hbm(cotangent), in_hbm(delta))
    return got[:halves], got[halves], got[halves + 1], got[halves + 2:]


def inner_kernel(rows, per_row, steps, *refs):
    tokens_hbm, weight_hbm, first_hbm, second_hbm, cot_hbm, low_weight_ref = refs[:6]
    cot_refs = refs[6:5 + rows]
    block_refs = refs[5 + rows:5 + rows + per_row]
    outs = refs[5 + rows + per_row:]
    new_weight_hbm, new_first_hbm, new_second_hbm, own_ref = outs[:4]
    message_refs = outs[4:3 + rows]
    tokens_ref, state_ref, fresh_ref, cot_ref, total_ref, turned_ref, sems, out_sems, cot_sem = refs[-9:]
    row = lax.axis_index("row")
    part = cot_ref.shape[0]
    tile = tokens_ref.shape[1] // steps
    block = [pl.ds(s * tile, tile) for s in range(steps)]
    states = (weight_hbm, first_hbm, second_hbm)
    fresh = (new_weight_hbm, new_first_hbm, new_second_hbm)

    cot_load = pltpu.make_async_copy(cot_hbm, cot_ref, cot_sem)
    token_loads, state_loads, stores = [], [], []
    for s in range(steps):
        token_loads.append(pltpu.make_async_copy(tokens_hbm.at[:, block[s]], tokens_ref.at[:, block[s]], sems.at[s, 3]))
        state_loads.append([
            pltpu.make_async_copy(state.at[block[s], :], state_ref.at[i, block[s], :], sems.at[s, i])
            for i, state in enumerate(states)
        ])
        stores.append([
            pltpu.make_async_copy(fresh_ref.at[i, block[s], :], out.at[block[s], :], out_sems.at[s, i])
            for i, out in enumerate(fresh)
        ])
    cot_load.start()
    for s in range(steps):
        token_loads[s].start()
        for load in state_loads[s]:
            load.start()

    size = block_refs[0].shape[0]
    for message_ref in message_refs:
        for k in range(per_row):
            message_ref[pl.ds(k * size, size), :] = block_refs[k][...]
    for k in range(1, rows):
        start = pl.multiple_of(mod(row - k, rows) * part, part)
        turned_ref[:, pl.ds(start, part)] = cot_refs[k - 1][...].T
    cot_load.wait()
    turned_ref[:, pl.ds(pl.multiple_of(row * part, part), part)] = cot_ref[...].T

    for s in range(steps):
        token_loads[s].wait()
        tokens = tokens_ref[:, block[s]]
        product = jnp.dot(tokens, low_weight_ref[block[s], :], preferred_element_type=jnp.float32)
        if s == 0:
            total_ref[...] = product
        else:
            total_ref[...] += product
        gradient = jnp.dot(turned_ref[...], tokens, preferred_element_type=jnp.float32).T
        for load in state_loads[s]:
            load.wait()
        weight = state_ref[0, block[s], :]
        first = BETA_ONE * state_ref[1, block[s], :] + (1.0 - BETA_ONE) * gradient
        second = BETA_TWO * state_ref[2, block[s], :] + (1.0 - BETA_TWO) * gradient * gradient
        fresh_ref[0, block[s], :] = weight - INNER_RATE * (
            first / (jnp.sqrt(second) + EPSILON) + WEIGHT_DECAY * weight
        )
        fresh_ref[1, block[s], :] = first
        fresh_ref[2, block[s], :] = second
        for store in stores[s]:
            store.start()

    own_ref[...] = total_ref[pl.ds(pl.multiple_of(row * part, part), part), :]
    for k in range(1, rows):
        start = pl.multiple_of(mod(row + k - rows, rows) * part, part)
        message_refs[k - 1][pl.ds(part, part), :] = total_ref[pl.ds(start, part), :].astype(jnp.bfloat16)
    for s in range(steps):
        for store in stores[s]:
            store.wait()


def inner(tokens, weight, first, second, cots, low_weight, blocks):
    rows, per_row = len(cots), len(blocks)
    count, depth = tokens.shape
    width = weight.shape[1]
    part = count // rows
    steps = depth // min(512, depth)
    full = jax.ShapeDtypeStruct((depth, width), jnp.float32)
    outs = [
        full,
        full,
        full,
        jax.ShapeDtypeStruct((part, width), jnp.float32),
    ] + [jax.ShapeDtypeStruct((2 * part, width), jnp.bfloat16)] * (rows - 1)
    got = pl.pallas_call(
        functools.partial(inner_kernel, rows, per_row, steps),
        in_specs=[HBM] * 5 + [WHOLE] * (rows + per_row),
        out_specs=[HBM] * 3 + [WHOLE] * rows,
        out_shape=outs,
        scratch_shapes=[
            pltpu.VMEM((count, depth), jnp.bfloat16),
            pltpu.VMEM((3, depth, width), jnp.float32),
            pltpu.VMEM((3, depth, width), jnp.float32),
            pltpu.VMEM((part, width), jnp.bfloat16),
            pltpu.VMEM((count, width), jnp.float32),
            pltpu.VMEM((width, count), jnp.bfloat16),
            pltpu.SemaphoreType.DMA((steps, 4)),
            pltpu.SemaphoreType.DMA((steps, 3)),
            pltpu.SemaphoreType.DMA,
        ],
        compiler_params=params(24),
        cost_estimate=pl.CostEstimate(
            flops=4 * count * depth * width, bytes_accessed=2 * count * depth + 24 * depth * width, transcendentals=0
        ),
        name="inner",
    )(*map(in_hbm, (tokens, weight, first, second, cots[0])), low_weight, *cots[1:], *blocks)
    return got[:3], got[3], got[4:]


def input_grad_kernel(rows, cols, *refs):
    per_row = cols // rows
    cot_refs, weight_refs = refs[:cols], refs[cols:2 * cols]
    out_ref, blocks_ref = refs[-2], refs[-1]
    row, col = lax.axis_index("row"), lax.axis_index("col")

    @pl.when(pl.program_id(0) == 0)
    def _():
        for j in range(rows):
            for k in range(per_row):
                block = mod(row - j, rows) * per_row + mod(lax.rem(col, per_row) - k, per_row)
                blocks_ref[block] = cot_refs[j * per_row + k][...]

    total = None
    pair = 2 if cols % 2 == 0 else 1
    for k in range(0, cols, pair):
        left = [blocks_ref[owner_of(col, k + i, cols)] for i in range(pair)]
        right = [weight_refs[k + i][...] for i in range(pair)]
        if pair > 1:
            left, right = [jnp.concatenate(left, axis=1)], [jnp.concatenate(right, axis=1)]
        piece = lax.dot_general(left[0], right[0], (((1,), (1,)), ((), ())), preferred_element_type=jnp.float32)
        total = piece if total is None else total + piece
    out_ref[...] = total.astype(jnp.bfloat16)


def input_grad_part(blocks, messages, weights, depth, half, before):
    per_row, rows, cols = len(blocks), len(messages) + 1, len(weights)
    chunk, width = blocks[0].shape
    tile = min(512, depth)
    steps = depth // tile
    aliased = [] if before is None else [before]
    in_specs, operands = [], []
    for source in [None] + list(messages):
        for k in range(per_row):
            in_specs.append(pl.BlockSpec((chunk, width), functools.partial(lambda k, d: (k, 0), 0 if source is None else k)))
            operands.append(blocks[k] if source is None else source)
    for array, part in weights:
        in_specs.append(pl.BlockSpec((tile, width), functools.partial(lambda first, d: (first + d, 0), part * steps)))
        operands.append(array)
    return pl.pallas_call(
        functools.partial(input_grad_kernel, rows, cols),
        grid=(steps,),
        in_specs=in_specs + [pl.BlockSpec(memory_space=pl.ANY)] * len(aliased),
        out_specs=pl.BlockSpec((chunk, tile), lambda d: (0, half * steps + d)),
        out_shape=jax.ShapeDtypeStruct((chunk, HALVES * depth), jnp.bfloat16),
        scratch_shapes=[pltpu.VMEM((cols, chunk, width), jnp.bfloat16)],
        input_output_aliases={2 * cols: 0} if aliased else {},
        compiler_params=params(16),
        cost_estimate=pl.CostEstimate(
            flops=2 * chunk * depth * width * cols, bytes_accessed=2 * (depth + chunk) * width * cols + 2 * chunk * depth,
            transcendentals=0,
        ),
        name="input_grad",
    )(*operands, *aliased)


def merge_kernel(replicas, slot_ref, sum_ref, other_ref, global_hbm, moment_hbm, new_global_hbm, new_outer_hbm, *scratch):
    global_ref, moment_ref, new_global_ref, new_outer_ref, sems = scratch
    slot = slot_ref[0]
    count = sum_ref.shape[0]
    slots = global_ref.shape[0] // count
    loads = [
        pltpu.make_async_copy(moment_hbm, moment_ref, sems.at[0]),
        pltpu.make_async_copy(global_hbm, global_ref, sems.at[1]),
    ]
    stores = [
        pltpu.make_async_copy(new_outer_ref, new_outer_hbm, sems.at[2]),
        pltpu.make_async_copy(new_global_ref, new_global_hbm, sems.at[3]),
    ]
    for load in loads:
        load.start()
    average = (sum_ref[...].astype(jnp.float32) + other_ref[...].astype(jnp.float32)) / replicas
    loads[0].wait()
    new_outer = NESTEROV * moment_ref[pl.ds(slot, count, stride=slots), :] + average
    new_outer_ref[...] = new_outer
    stores[0].start()
    loads[1].wait()
    held = global_ref[pl.ds(slot, count, stride=slots), :]
    new_global_ref[...] = held - OUTER_RATE * (average + NESTEROV * new_outer)
    stores[1].start()
    for store in stores:
        store.wait()


def interleaved(x):
    slots, size = x.shape
    return x.reshape(slots, size // LANES, LANES).transpose(1, 0, 2).reshape(slots * size // LANES, LANES)


def outer_sums(low, axis):
    n = lax.axis_size(axis)
    if not is_power_of_two(n):
        return lax.psum(low, axis), jnp.zeros_like(low)
    bit = 1
    while True:
        other = lax.ppermute(low, axis, swap_pairs(n, bit))
        bit *= 2
        if bit >= n:
            return low, other
        low = (low.astype(jnp.float32) + other.astype(jnp.float32)).astype(jnp.bfloat16)


def merge(low, other, global_params, outer_moment, group_slot, replicas):
    shape = jax.ShapeDtypeStruct(low.shape, jnp.float32)
    new_global, new_outer = pl.pallas_call(
        functools.partial(merge_kernel, replicas),
        out_shape=[shape, shape],
        in_specs=[pl.BlockSpec(memory_space=pltpu.SMEM)] + [WHOLE] * 2 + [HBM] * 2,
        out_specs=[HBM] * 2,
        scratch_shapes=[pltpu.VMEM((global_params.size // LANES, LANES), jnp.float32)] * 2
        + [pltpu.VMEM(low.shape, jnp.float32)] * 2
        + [pltpu.SemaphoreType.DMA((4,))],
        compiler_params=params(16),
        cost_estimate=pl.CostEstimate(flops=8 * low.size, bytes_accessed=28 * low.size, transcendentals=0),
        name="merge",
    )(group_slot, low, other, in_hbm(interleaved(global_params)), in_hbm(interleaved(outer_moment)))
    return new_global.reshape(-1), new_outer.reshape(-1)


def on_device(
    tokens,
    cotangent,
    weight,
    first_moment,
    second_moment,
    outer_delta,
    global_params,
    outer_moment,
    group_slot,
):
    rows, cols = lax.axis_size("row"), lax.axis_size("col")
    replicas = lax.axis_size("rep")
    per_row = cols // rows
    depth = weight.shape[1] // HALVES
    cots = shifted(cotangent, "row")
    halves, whole, low, chunks = prepare(weight[0], cotangent, outer_delta.reshape(-1, LANES), per_row, HALVES)
    received = [lax.ppermute(chunks[k], ("row", "col"), chunk_pairs(rows, cols, per_row, k)) for k in range(per_row)]
    weights = gather_halves(halves, whole, "col")

    (new_weight, new_first, new_second), own, messages = inner(
        tokens, weight[0], first_moment[0], second_moment[0], cots, whole, received
    )
    messages = [lax.ppermute(m, "row", shift_pairs(rows, k + 1)) for k, m in enumerate(messages)]
    low, received = after(low, received)
    low, other = outer_sums(low, "rep")
    new_global, new_outer = merge(low, other, global_params, outer_moment, group_slot, replicas)

    keys_values = own
    for message in messages:
        keys_values += message[own.shape[0]:].astype(jnp.float32)
    keys_values = keys_values.astype(jnp.bfloat16)

    input_grad = None
    for half in range(HALVES):
        input_grad = input_grad_part(received, messages, weights[half], depth, half, input_grad)
    return (keys_values, input_grad, new_weight[None], new_first[None], new_second[None], new_global, new_outer)


def solution(mesh):
    in_specs = (
        P("rep", "row"),
        P(("rep", "row"), "col"),
        P("rep", "row", "col"),
        P("rep", "row", "col"),
        P("rep", "row", "col"),
        P("rep", ("row", "col")),
        P(None, ("row", "col")),
        P(None, ("row", "col")),
        P(),
    )
    out_specs = (
        P(("rep", "row"), "col"),
        P(("rep", "col"), "row"),
        P("rep", "row", "col"),
        P("rep", "row", "col"),
        P("rep", "row", "col"),
        P(("row", "col")),
        P(("row", "col")),
    )
    return jax.shard_map(
        on_device, mesh=mesh, in_specs=in_specs, out_specs=out_specs, check_vma=False
    )
```

```python
import functools

import jax
import jax.numpy as jnp
from jax import lax
from jax.experimental import pallas as pl
from jax.experimental.pallas import tpu as pltpu
from jax.sharding import PartitionSpec as P

BETA_ONE = 0.9
BETA_TWO = 0.95
INNER_RATE = 0.0003
WEIGHT_DECAY = 0.1
EPSILON = 1e-08
OUTER_RATE = 0.7
NESTEROV = 0.9
LANES = 128

WHOLE = pl.BlockSpec(memory_space=pltpu.VMEM)
HBM = pl.BlockSpec(memory_space=pltpu.HBM)


def params(mebibytes):
    return pltpu.CompilerParams(vmem_limit_bytes=mebibytes * 1024 * 1024)


def after(x, others):
    return lax.optimization_barrier((x, others))


def in_hbm(x):
    return pltpu.with_memory_space_constraint(x, pltpu.HBM)


def is_power_of_two(n):
    return n & (n - 1) == 0


def swap_pairs(n, bit):
    return [(i, i ^ bit) for i in range(n)]


def shift_pairs(n, k):
    return [(i, (i + k) % n) for i in range(n)]


def mod(value, n):
    return lax.rem(value + n, n)


def gather_offsets(block, axis, early):
    n = lax.axis_size(axis)
    have = {0: block}
    if is_power_of_two(n):
        bit = n // 2
        while bit:
            for k in list(have):
                if k:
                    have[k], _ = after(have[k], (early, have[bit]))
                have[k ^ bit] = lax.ppermute(have[k], axis, swap_pairs(n, bit))
            bit //= 2
    else:
        for k in range(1, n):
            have[k] = lax.ppermute(have[k - 1], axis, shift_pairs(n, n - 1))
    return [have[k] for k in range(n)]


def owner_of(me, k, n):
    return me ^ k if is_power_of_two(n) else mod(me + k, n)


def shifted(block, axis):
    n = lax.axis_size(axis)
    return [block] + [lax.ppermute(block, axis, shift_pairs(n, k)) for k in range(1, n)]


def chunk_pairs(rows, cols, per_row, k):
    pairs = []
    for r in range(rows):
        for c in range(cols):
            pairs.append((r * cols + c, (c // per_row) * cols + r * per_row + (c + k) % per_row))
    return pairs


def prepare_kernel(per_row, weight_hbm, cot_hbm, delta_hbm, low_weight_ref, low_delta_ref, *refs):
    chunk_refs = refs[:per_row]
    weight_ref, delta_ref, sems, chunk_sems = refs[per_row:]
    size = chunk_refs[0].shape[0]
    col = lax.axis_index("col")
    loads = [
        pltpu.make_async_copy(weight_hbm, weight_ref, sems.at[0]),
        pltpu.make_async_copy(delta_hbm, delta_ref, sems.at[1]),
    ]
    chunks = []
    for k in range(per_row):
        start = pl.multiple_of(lax.rem(col + k, per_row) * size, size)
        chunks.append(pltpu.make_async_copy(cot_hbm.at[pl.ds(start, size), :], chunk_refs[k], chunk_sems.at[k]))
    for copy in loads + chunks:
        copy.start()
    loads[0].wait()
    low_weight_ref[...] = weight_ref[...].astype(jnp.bfloat16)
    loads[1].wait()
    low_delta_ref[...] = delta_ref[...].astype(jnp.bfloat16)
    for copy in chunks:
        copy.wait()


def prepare(weight, cotangent, delta, per_row):
    chunk = cotangent.shape[0] // per_row
    shape = lambda *s: jax.ShapeDtypeStruct(s, jnp.bfloat16)
    outs = [shape(*weight.shape), shape(*delta.shape)] + [shape(chunk, cotangent.shape[1])] * per_row
    got = pl.pallas_call(
        functools.partial(prepare_kernel, per_row),
        out_shape=outs,
        in_specs=[HBM] * 3,
        out_specs=[WHOLE] * len(outs),
        scratch_shapes=[
            pltpu.VMEM(weight.shape, jnp.float32),
            pltpu.VMEM(delta.shape, jnp.float32),
            pltpu.SemaphoreType.DMA((2,)),
            pltpu.SemaphoreType.DMA((per_row,)),
        ],
        compiler_params=params(16),
        cost_estimate=pl.CostEstimate(flops=0, bytes_accessed=8 * weight.size, transcendentals=0),
        name="prepare",
    )(*map(in_hbm, (weight, cotangent, delta)))
    return got[0], got[1], got[2:]


def pack_kernel(per_row, *refs):
    block_refs, sum_refs = refs[:per_row], refs[per_row:per_row + (len(refs) - per_row) // 2]
    out_refs = refs[per_row + len(sum_refs):]
    size, part = block_refs[0].shape[0], sum_refs[0].shape[0]
    for out_ref, sum_ref in zip(out_refs, sum_refs):
        for k in range(per_row):
            out_ref[pl.ds(k * size, size), :] = block_refs[k][...]
        out_ref[pl.ds(part, part), :] = sum_ref[...]


def pack(blocks, sends):
    part, width = sends[0].shape
    return pl.pallas_call(
        functools.partial(pack_kernel, len(blocks)),
        out_shape=[jax.ShapeDtypeStruct((2 * part, width), jnp.bfloat16)] * len(sends),
        in_specs=[WHOLE] * (len(blocks) + len(sends)),
        out_specs=[WHOLE] * len(sends),
        compiler_params=params(16),
        cost_estimate=pl.CostEstimate(flops=0, bytes_accessed=8 * part * width, transcendentals=0),
        name="pack",
    )(*blocks, *sends)


def inner_kernel(rows, steps, *refs):
    tokens_hbm, weight_hbm, first_hbm, second_hbm, cot_hbm, low_weight_ref = refs[:6]
    cot_refs = refs[6:5 + rows]
    new_weight_hbm, new_first_hbm, new_second_hbm, own_ref = refs[5 + rows:9 + rows]
    send_refs = refs[9 + rows:8 + 2 * rows]
    tokens_ref, state_ref, fresh_ref, cot_ref, total_ref, turned_ref, sems, out_sems, cot_sem = refs[-9:]
    row = lax.axis_index("row")
    part = cot_ref.shape[0]
    tile = tokens_ref.shape[1] // steps
    block = [pl.ds(s * tile, tile) for s in range(steps)]
    states = (weight_hbm, first_hbm, second_hbm)
    fresh = (new_weight_hbm, new_first_hbm, new_second_hbm)

    cot_load = pltpu.make_async_copy(cot_hbm, cot_ref, cot_sem)
    token_loads, state_loads, stores = [], [], []
    for s in range(steps):
        token_loads.append(pltpu.make_async_copy(tokens_hbm.at[:, block[s]], tokens_ref.at[:, block[s]], sems.at[s, 3]))
        state_loads.append([
            pltpu.make_async_copy(state.at[block[s], :], state_ref.at[i, block[s], :], sems.at[s, i])
            for i, state in enumerate(states)
        ])
        stores.append([
            pltpu.make_async_copy(fresh_ref.at[i, block[s], :], out.at[block[s], :], out_sems.at[s, i])
            for i, out in enumerate(fresh)
        ])
    cot_load.start()
    for s in range(steps):
        token_loads[s].start()
        for load in state_loads[s]:
            load.start()

    for k in range(1, rows):
        start = pl.multiple_of(mod(row - k, rows) * part, part)
        turned_ref[:, pl.ds(start, part)] = cot_refs[k - 1][...].T
    cot_load.wait()
    turned_ref[:, pl.ds(pl.multiple_of(row * part, part), part)] = cot_ref[...].T

    for s in range(steps):
        token_loads[s].wait()
        tokens = tokens_ref[:, block[s]]
        product = jnp.dot(tokens, low_weight_ref[block[s], :], preferred_element_type=jnp.float32)
        if s == 0:
            total_ref[...] = product
        else:
            total_ref[...] += product
        gradient = jnp.dot(turned_ref[...], tokens, preferred_element_type=jnp.float32).T
        for load in state_loads[s]:
            load.wait()
        weight = state_ref[0, block[s], :]
        first = BETA_ONE * state_ref[1, block[s], :] + (1.0 - BETA_ONE) * gradient
        second = BETA_TWO * state_ref[2, block[s], :] + (1.0 - BETA_TWO) * gradient * gradient
        fresh_ref[0, block[s], :] = weight - INNER_RATE * (
            first / (jnp.sqrt(second) + EPSILON) + WEIGHT_DECAY * weight
        )
        fresh_ref[1, block[s], :] = first
        fresh_ref[2, block[s], :] = second
        for store in stores[s]:
            store.start()

    own_ref[...] = total_ref[pl.ds(pl.multiple_of(row * part, part), part), :]
    for k in range(1, rows):
        start = pl.multiple_of(mod(row + k - rows, rows) * part, part)
        send_refs[k - 1][...] = total_ref[pl.ds(start, part), :].astype(jnp.bfloat16)
    for s in range(steps):
        for store in stores[s]:
            store.wait()


def inner(tokens, weight, first, second, cots, low_weight):
    rows = len(cots)
    count, depth = tokens.shape
    width = weight.shape[1]
    part = count // rows
    steps = depth // min(512, depth)
    full = jax.ShapeDtypeStruct((depth, width), jnp.float32)
    outs = [
        full,
        full,
        full,
        jax.ShapeDtypeStruct((part, width), jnp.float32),
    ] + [jax.ShapeDtypeStruct((part, width), jnp.bfloat16)] * (rows - 1)
    got = pl.pallas_call(
        functools.partial(inner_kernel, rows, steps),
        in_specs=[HBM] * 5 + [WHOLE] * rows,
        out_specs=[HBM] * 3 + [WHOLE] * rows,
        out_shape=outs,
        scratch_shapes=[
            pltpu.VMEM((count, depth), jnp.bfloat16),
            pltpu.VMEM((3, depth, width), jnp.float32),
            pltpu.VMEM((3, depth, width), jnp.float32),
            pltpu.VMEM((part, width), jnp.bfloat16),
            pltpu.VMEM((count, width), jnp.float32),
            pltpu.VMEM((width, count), jnp.bfloat16),
            pltpu.SemaphoreType.DMA((steps, 4)),
            pltpu.SemaphoreType.DMA((steps, 3)),
            pltpu.SemaphoreType.DMA,
        ],
        compiler_params=params(24),
        cost_estimate=pl.CostEstimate(
            flops=4 * count * depth * width, bytes_accessed=2 * count * depth + 24 * depth * width, transcendentals=0
        ),
        name="inner",
    )(*map(in_hbm, (tokens, weight, first, second, cots[0])), low_weight, *cots[1:])
    return got[:3], got[3], got[4:]


def times_transposed(left, right):
    return lax.dot_general(left, right, (((1,), (1,)), ((), ())), preferred_element_type=jnp.float32)


def arrived_kernel(rows, cols, tile, *refs):
    per_row = cols // rows
    block_refs, message_refs = refs[:per_row], refs[per_row:per_row + rows - 1]
    own_ref = refs[per_row + rows - 1]
    weight_refs = refs[per_row + rows:per_row + rows + cols - 1]
    sum_ref, last_ref, keys_values_hbm, blocks_ref, keys_values_ref, sem = refs[-6:]
    row, col = lax.axis_index("row"), lax.axis_index("col")
    size, part = block_refs[0].shape[0], own_ref.shape[0]
    total = own_ref[...]
    for message_ref in message_refs:
        total += message_ref[pl.ds(part, part), :].astype(jnp.float32)
    keys_values_ref[...] = total.astype(jnp.bfloat16)
    store = pltpu.make_async_copy(keys_values_ref, keys_values_hbm, sem)
    store.start()
    for k in range(per_row):
        column = mod(lax.rem(col, per_row) - k, per_row)
        blocks_ref[row * per_row + column] = block_refs[k][...]
        for j in range(1, rows):
            blocks_ref[mod(row - j, rows) * per_row + column] = message_refs[j - 1][pl.ds(k * size, size), :]
    last_ref[...] = blocks_ref[owner_of(col, cols - 1, cols)]
    left = [blocks_ref[owner_of(col, k, cols)] for k in range(cols - 1)]
    for start in range(0, weight_refs[0].shape[0], tile):
        features = pl.ds(start, tile)
        piece = None
        for k in range(0, cols - 1, 2):
            few = range(k, min(k + 2, cols - 1))
            product = times_transposed(
                jnp.concatenate([left[i] for i in few], axis=1),
                jnp.concatenate([weight_refs[i][features, :] for i in few], axis=1),
            )
            piece = product if piece is None else piece + product
        sum_ref[:, features] = piece
    store.wait()


def arrived(blocks, messages, own, weights, cols):
    rows, per_row = len(messages) + 1, len(blocks)
    size, width = blocks[0].shape
    depth = weights[0].shape[0]
    return pl.pallas_call(
        functools.partial(arrived_kernel, rows, cols, min(512, depth)),
        out_shape=[
            jax.ShapeDtypeStruct((size, depth), jnp.float32),
            jax.ShapeDtypeStruct((size, width), jnp.bfloat16),
            jax.ShapeDtypeStruct(own.shape, jnp.bfloat16),
        ],
        in_specs=[WHOLE] * (per_row + rows + cols - 1),
        out_specs=[WHOLE, WHOLE, HBM],
        scratch_shapes=[
            pltpu.VMEM((cols, size, width), jnp.bfloat16),
            pltpu.VMEM(own.shape, jnp.bfloat16),
            pltpu.SemaphoreType.DMA,
        ],
        compiler_params=params(24),
        cost_estimate=pl.CostEstimate(
            flops=2 * size * depth * width * (cols - 1), bytes_accessed=4 * size * depth, transcendentals=0
        ),
        name="arrived",
    )(*blocks, *messages, own, *weights)


def finish_kernel(tile, sum_ref, block_ref, weight_ref, out_hbm, out_ref, sems):
    stores = []
    for i, start in enumerate(range(0, weight_ref.shape[0], tile)):
        features = pl.ds(start, tile)
        piece = times_transposed(block_ref[...], weight_ref[features, :])
        out_ref[:, features] = (sum_ref[:, features] + piece).astype(jnp.bfloat16)
        stores.append(pltpu.make_async_copy(out_ref.at[:, features], out_hbm.at[:, features], sems.at[i]))
        stores[-1].start()
    for store in stores:
        store.wait()


def finish(total, block, weight):
    size, depth = total.shape
    tile = min(512, depth)
    return pl.pallas_call(
        functools.partial(finish_kernel, tile),
        out_shape=jax.ShapeDtypeStruct((size, depth), jnp.bfloat16),
        in_specs=[WHOLE] * 3,
        out_specs=HBM,
        scratch_shapes=[pltpu.VMEM((size, depth), jnp.bfloat16), pltpu.SemaphoreType.DMA((depth // tile,))],
        compiler_params=params(16),
        cost_estimate=pl.CostEstimate(
            flops=2 * size * depth * block.shape[1], bytes_accessed=6 * size * depth, transcendentals=0
        ),
        name="finish",
    )(total, block, weight)


def merge_kernel(replicas, slot_ref, sum_ref, other_ref, global_hbm, moment_hbm, new_global_hbm, new_outer_hbm, *scratch):
    global_ref, moment_ref, new_global_ref, new_outer_ref, sems = scratch
    slot = slot_ref[0]
    count = sum_ref.shape[0]
    slots = global_ref.shape[0] // count
    loads = [
        pltpu.make_async_copy(moment_hbm, moment_ref, sems.at[0]),
        pltpu.make_async_copy(global_hbm, global_ref, sems.at[1]),
    ]
    stores = [
        pltpu.make_async_copy(new_outer_ref, new_outer_hbm, sems.at[2]),
        pltpu.make_async_copy(new_global_ref, new_global_hbm, sems.at[3]),
    ]
    for load in loads:
        load.start()
    average = (sum_ref[...].astype(jnp.float32) + other_ref[...].astype(jnp.float32)) / replicas
    loads[0].wait()
    new_outer = NESTEROV * moment_ref[pl.ds(slot, count, stride=slots), :] + average
    new_outer_ref[...] = new_outer
    stores[0].start()
    loads[1].wait()
    held = global_ref[pl.ds(slot, count, stride=slots), :]
    new_global_ref[...] = held - OUTER_RATE * (average + NESTEROV * new_outer)
    stores[1].start()
    for store in stores:
        store.wait()


def interleaved(x):
    slots, size = x.shape
    return x.reshape(slots, size // LANES, LANES).transpose(1, 0, 2).reshape(slots * size // LANES, LANES)


def outer_sums(low, axis, early):
    n = lax.axis_size(axis)
    if not is_power_of_two(n):
        return lax.psum(low, axis), jnp.zeros_like(low)
    bit = 1
    while True:
        other = lax.ppermute(low, axis, swap_pairs(n, bit))
        bit *= 2
        if bit >= n:
            return low, other
        other, _ = after(other, early)
        low = (low.astype(jnp.float32) + other.astype(jnp.float32)).astype(jnp.bfloat16)


def merge(low, other, global_params, outer_moment, group_slot, replicas):
    shape = jax.ShapeDtypeStruct(low.shape, jnp.float32)
    new_global, new_outer = pl.pallas_call(
        functools.partial(merge_kernel, replicas),
        out_shape=[shape, shape],
        in_specs=[pl.BlockSpec(memory_space=pltpu.SMEM)] + [WHOLE] * 2 + [HBM] * 2,
        out_specs=[HBM] * 2,
        scratch_shapes=[pltpu.VMEM((global_params.size // LANES, LANES), jnp.float32)] * 2
        + [pltpu.VMEM(low.shape, jnp.float32)] * 2
        + [pltpu.SemaphoreType.DMA((4,))],
        compiler_params=params(16),
        cost_estimate=pl.CostEstimate(flops=8 * low.size, bytes_accessed=28 * low.size, transcendentals=0),
        name="merge",
    )(group_slot, low, other, in_hbm(interleaved(global_params)), in_hbm(interleaved(outer_moment)))
    return new_global.reshape(-1), new_outer.reshape(-1)


def on_device(
    tokens,
    cotangent,
    weight,
    first_moment,
    second_moment,
    outer_delta,
    global_params,
    outer_moment,
    group_slot,
):
    rows, cols = lax.axis_size("row"), lax.axis_size("col")
    replicas = lax.axis_size("rep")
    per_row = cols // rows
    cots = shifted(cotangent, "row")
    low_weight, low, chunks = prepare(weight[0], cotangent, outer_delta.reshape(-1, LANES), per_row)
    received = [lax.ppermute(chunks[k], ("row", "col"), chunk_pairs(rows, cols, per_row, k)) for k in range(per_row)]
    (new_weight, new_first, new_second), own, sends = inner(
        tokens, weight[0], first_moment[0], second_moment[0], cots, low_weight
    )
    weights = gather_offsets(low_weight, "col", sends)
    low, other = outer_sums(low, "rep", (sends, weights[1], weights[cols // 2]))
    received, _ = after(received, weights[cols // 2])
    messages = [lax.ppermute(m, "row", shift_pairs(rows, k + 1)) for k, m in enumerate(pack(received, sends))]
    total, block, keys_values = arrived(received, messages, own, weights[:-1], cols)
    other, _ = after(other, total)
    new_global, new_outer = merge(low, other, global_params, outer_moment, group_slot, replicas)
    last, _ = after(weights[-1], (new_outer, total))
    input_grad = finish(total, block, last)
    return (keys_values, input_grad, new_weight[None], new_first[None], new_second[None], new_global, new_outer)


def solution(mesh):
    in_specs = (
        P("rep", "row"),
        P(("rep", "row"), "col"),
        P("rep", "row", "col"),
        P("rep", "row", "col"),
        P("rep", "row", "col"),
        P("rep", ("row", "col")),
        P(None, ("row", "col")),
        P(None, ("row", "col")),
        P(),
    )
    out_specs = (
        P(("rep", "row"), "col"),
        P(("rep", "col"), "row"),
        P("rep", "row", "col"),
        P("rep", "row", "col"),
        P("rep", "row", "col"),
        P(("row", "col")),
        P(("row", "col")),
    )
    return jax.shard_map(
        on_device, mesh=mesh, in_specs=in_specs, out_specs=out_specs, check_vma=False
    )
```

```python
import functools

import jax
import jax.numpy as jnp
from jax import lax
from jax.experimental import pallas as pl
from jax.experimental.pallas import tpu as pltpu
from jax.sharding import PartitionSpec as P

BETA_ONE = 0.9
BETA_TWO = 0.95
INNER_RATE = 0.0003
WEIGHT_DECAY = 0.1
EPSILON = 1e-08
OUTER_RATE = 0.7
NESTEROV = 0.9
LANES = 128

WHOLE = pl.BlockSpec(memory_space=pltpu.VMEM)
HBM = pl.BlockSpec(memory_space=pltpu.HBM)


def params(mebibytes):
    return pltpu.CompilerParams(vmem_limit_bytes=mebibytes * 1024 * 1024)


def after(x, others):
    return lax.optimization_barrier((x, others))


def in_hbm(x):
    return pltpu.with_memory_space_constraint(x, pltpu.HBM)


def is_power_of_two(n):
    return n & (n - 1) == 0


def swap_pairs(n, bit):
    return [(i, i ^ bit) for i in range(n)]


def shift_pairs(n, k):
    return [(i, (i + k) % n) for i in range(n)]


def mod(value, n):
    return lax.rem(value + n, n)


def gather_offsets(block, axis, early):
    n = lax.axis_size(axis)
    have = {0: block}
    if is_power_of_two(n):
        bit = n // 2
        while bit:
            for k in list(have):
                if k:
                    have[k], _ = after(have[k], early)
                have[k ^ bit] = lax.ppermute(have[k], axis, swap_pairs(n, bit))
            bit //= 2
    else:
        for k in range(1, n):
            have[k] = lax.ppermute(have[k - 1], axis, shift_pairs(n, n - 1))
    return [have[k] for k in range(n)]


def owner_of(me, k, n):
    return me ^ k if is_power_of_two(n) else mod(me + k, n)


def shifted(block, axis):
    n = lax.axis_size(axis)
    return [block] + [lax.ppermute(block, axis, shift_pairs(n, k)) for k in range(1, n)]


def chunk_pairs(rows, cols, per_row, k):
    pairs = []
    for r in range(rows):
        for c in range(cols):
            pairs.append((r * cols + c, (c // per_row) * cols + r * per_row + (c + k) % per_row))
    return pairs


def prepare_kernel(per_row, weight_hbm, cot_hbm, delta_hbm, low_weight_ref, low_delta_ref, *refs):
    chunk_refs = refs[:per_row]
    weight_ref, delta_ref, sems, chunk_sems = refs[per_row:]
    size = chunk_refs[0].shape[0]
    col = lax.axis_index("col")
    loads = [
        pltpu.make_async_copy(weight_hbm, weight_ref, sems.at[0]),
        pltpu.make_async_copy(delta_hbm, delta_ref, sems.at[1]),
    ]
    chunks = []
    for k in range(per_row):
        start = pl.multiple_of(lax.rem(col + k, per_row) * size, size)
        chunks.append(pltpu.make_async_copy(cot_hbm.at[pl.ds(start, size), :], chunk_refs[k], chunk_sems.at[k]))
    for copy in loads + chunks:
        copy.start()
    loads[0].wait()
    low_weight_ref[...] = weight_ref[...].astype(jnp.bfloat16)
    loads[1].wait()
    low_delta_ref[...] = delta_ref[...].astype(jnp.bfloat16)
    for copy in chunks:
        copy.wait()


def prepare(weight, cotangent, delta, per_row):
    chunk = cotangent.shape[0] // per_row
    shape = lambda *s: jax.ShapeDtypeStruct(s, jnp.bfloat16)
    outs = [shape(*weight.shape), shape(*delta.shape)] + [shape(chunk, cotangent.shape[1])] * per_row
    got = pl.pallas_call(
        functools.partial(prepare_kernel, per_row),
        out_shape=outs,
        in_specs=[HBM] * 3,
        out_specs=[WHOLE] * len(outs),
        scratch_shapes=[
            pltpu.VMEM(weight.shape, jnp.float32),
            pltpu.VMEM(delta.shape, jnp.float32),
            pltpu.SemaphoreType.DMA((2,)),
            pltpu.SemaphoreType.DMA((per_row,)),
        ],
        compiler_params=params(16),
        cost_estimate=pl.CostEstimate(flops=0, bytes_accessed=8 * weight.size, transcendentals=0),
        name="prepare",
    )(*map(in_hbm, (weight, cotangent, delta)))
    return got[0], got[1], got[2:]


def pack_kernel(per_row, *refs):
    block_refs, sum_refs = refs[:per_row], refs[per_row:per_row + (len(refs) - per_row) // 2]
    out_refs = refs[per_row + len(sum_refs):]
    size, part = block_refs[0].shape[0], sum_refs[0].shape[0]
    for out_ref, sum_ref in zip(out_refs, sum_refs):
        for k in range(per_row):
            out_ref[pl.ds(k * size, size), :] = block_refs[k][...]
        out_ref[pl.ds(part, part), :] = sum_ref[...]


def pack(blocks, sends):
    part, width = sends[0].shape
    return pl.pallas_call(
        functools.partial(pack_kernel, len(blocks)),
        out_shape=[jax.ShapeDtypeStruct((2 * part, width), jnp.bfloat16)] * len(sends),
        in_specs=[WHOLE] * (len(blocks) + len(sends)),
        out_specs=[WHOLE] * len(sends),
        compiler_params=params(16),
        cost_estimate=pl.CostEstimate(flops=0, bytes_accessed=8 * part * width, transcendentals=0),
        name="pack",
    )(*blocks, *sends)


def inner_kernel(rows, steps, *refs):
    tokens_hbm, weight_hbm, first_hbm, second_hbm, cot_hbm, low_weight_ref = refs[:6]
    cot_refs = refs[6:5 + rows]
    new_weight_hbm, new_first_hbm, new_second_hbm, own_ref = refs[5 + rows:9 + rows]
    send_refs = refs[9 + rows:8 + 2 * rows]
    tokens_ref, state_ref, fresh_ref, cot_ref, total_ref, turned_ref, sems, out_sems, cot_sem = refs[-9:]
    row = lax.axis_index("row")
    part = cot_ref.shape[0]
    tile = tokens_ref.shape[1] // steps
    block = [pl.ds(s * tile, tile) for s in range(steps)]
    states = (weight_hbm, first_hbm, second_hbm)
    fresh = (new_weight_hbm, new_first_hbm, new_second_hbm)

    cot_load = pltpu.make_async_copy(cot_hbm, cot_ref, cot_sem)
    token_loads, state_loads, stores = [], [], []
    for s in range(steps):
        token_loads.append(pltpu.make_async_copy(tokens_hbm.at[:, block[s]], tokens_ref.at[:, block[s]], sems.at[s, 3]))
        state_loads.append([
            pltpu.make_async_copy(state.at[block[s], :], state_ref.at[i, block[s], :], sems.at[s, i])
            for i, state in enumerate(states)
        ])
        stores.append([
            pltpu.make_async_copy(fresh_ref.at[i, block[s], :], out.at[block[s], :], out_sems.at[s, i])
            for i, out in enumerate(fresh)
        ])
    cot_load.start()
    for s in range(steps):
        token_loads[s].start()
        for load in state_loads[s]:
            load.start()

    for k in range(1, rows):
        start = pl.multiple_of(mod(row - k, rows) * part, part)
        turned_ref[:, pl.ds(start, part)] = cot_refs[k - 1][...].T
    cot_load.wait()
    turned_ref[:, pl.ds(pl.multiple_of(row * part, part), part)] = cot_ref[...].T

    for s in range(steps):
        token_loads[s].wait()
        tokens = tokens_ref[:, block[s]]
        product = jnp.dot(tokens, low_weight_ref[block[s], :], preferred_element_type=jnp.float32)
        if s == 0:
            total_ref[...] = product
        else:
            total_ref[...] += product
        gradient = jnp.dot(turned_ref[...], tokens, preferred_element_type=jnp.float32).T
        for load in state_loads[s]:
            load.wait()
        weight = state_ref[0, block[s], :]
        first = BETA_ONE * state_ref[1, block[s], :] + (1.0 - BETA_ONE) * gradient
        second = BETA_TWO * state_ref[2, block[s], :] + (1.0 - BETA_TWO) * gradient * gradient
        fresh_ref[0, block[s], :] = weight - INNER_RATE * (
            first / (jnp.sqrt(second) + EPSILON) + WEIGHT_DECAY * weight
        )
        fresh_ref[1, block[s], :] = first
        fresh_ref[2, block[s], :] = second
        for store in stores[s]:
            store.start()

    own_ref[...] = total_ref[pl.ds(pl.multiple_of(row * part, part), part), :]
    for k in range(1, rows):
        start = pl.multiple_of(mod(row + k - rows, rows) * part, part)
        send_refs[k - 1][...] = total_ref[pl.ds(start, part), :].astype(jnp.bfloat16)
    for s in range(steps):
        for store in stores[s]:
            store.wait()


def inner(tokens, weight, first, second, cots, low_weight):
    rows = len(cots)
    count, depth = tokens.shape
    width = weight.shape[1]
    part = count // rows
    steps = depth // min(512, depth)
    full = jax.ShapeDtypeStruct((depth, width), jnp.float32)
    outs = [
        full,
        full,
        full,
        jax.ShapeDtypeStruct((part, width), jnp.float32),
    ] + [jax.ShapeDtypeStruct((part, width), jnp.bfloat16)] * (rows - 1)
    got = pl.pallas_call(
        functools.partial(inner_kernel, rows, steps),
        in_specs=[HBM] * 5 + [WHOLE] * rows,
        out_specs=[HBM] * 3 + [WHOLE] * rows,
        out_shape=outs,
        scratch_shapes=[
            pltpu.VMEM((count, depth), jnp.bfloat16),
            pltpu.VMEM((3, depth, width), jnp.float32),
            pltpu.VMEM((3, depth, width), jnp.float32),
            pltpu.VMEM((part, width), jnp.bfloat16),
            pltpu.VMEM((count, width), jnp.float32),
            pltpu.VMEM((width, count), jnp.bfloat16),
            pltpu.SemaphoreType.DMA((steps, 4)),
            pltpu.SemaphoreType.DMA((steps, 3)),
            pltpu.SemaphoreType.DMA,
        ],
        compiler_params=params(24),
        cost_estimate=pl.CostEstimate(
            flops=4 * count * depth * width, bytes_accessed=2 * count * depth + 24 * depth * width, transcendentals=0
        ),
        name="inner",
    )(*map(in_hbm, (tokens, weight, first, second, cots[0])), low_weight, *cots[1:])
    return got[:3], got[3], got[4:]


def times_transposed(left, right):
    return lax.dot_general(left, right, (((1,), (1,)), ((), ())), preferred_element_type=jnp.float32)


def arrived_kernel(rows, cols, tile, *refs):
    per_row = cols // rows
    block_refs, message_refs = refs[:per_row], refs[per_row:per_row + rows - 1]
    own_ref = refs[per_row + rows - 1]
    weight_refs = refs[per_row + rows:per_row + rows + cols - 1]
    slot_ref, global_hbm, moment_hbm, sum_ref, last_ref, held_ref, prior_ref, keys_values_hbm = refs[-14:-6]
    blocks_ref, keys_values_ref, global_ref, moment_ref, sem, slot_sems = refs[-6:]
    row, col = lax.axis_index("row"), lax.axis_index("col")
    loads = [
        pltpu.make_async_copy(global_hbm, global_ref, slot_sems.at[0]),
        pltpu.make_async_copy(moment_hbm, moment_ref, slot_sems.at[1]),
    ]
    for load in loads:
        load.start()
    size, part = block_refs[0].shape[0], own_ref.shape[0]
    total = own_ref[...]
    for message_ref in message_refs:
        total += message_ref[pl.ds(part, part), :].astype(jnp.float32)
    keys_values_ref[...] = total.astype(jnp.bfloat16)
    store = pltpu.make_async_copy(keys_values_ref, keys_values_hbm, sem)
    store.start()
    for k in range(per_row):
        column = mod(lax.rem(col, per_row) - k, per_row)
        blocks_ref[row * per_row + column] = block_refs[k][...]
        for j in range(1, rows):
            blocks_ref[mod(row - j, rows) * per_row + column] = message_refs[j - 1][pl.ds(k * size, size), :]
    last_ref[...] = blocks_ref[owner_of(col, cols - 1, cols)]
    left = [blocks_ref[owner_of(col, k, cols)] for k in range(cols - 1)]
    for start in range(0, weight_refs[0].shape[0], tile):
        features = pl.ds(start, tile)
        piece = None
        for k in range(0, cols - 1, 2):
            few = range(k, min(k + 2, cols - 1))
            product = times_transposed(
                jnp.concatenate([left[i] for i in few], axis=1),
                jnp.concatenate([weight_refs[i][features, :] for i in few], axis=1),
            )
            piece = product if piece is None else piece + product
        sum_ref[:, features] = piece
    slot, count = slot_ref[0], held_ref.shape[0]
    slots = global_ref.shape[0] // count
    for load, source_ref, out_ref in zip(loads, (global_ref, moment_ref), (held_ref, prior_ref)):
        load.wait()
        out_ref[...] = source_ref[pl.ds(slot, count, stride=slots), :]
    store.wait()


def arrived(blocks, messages, own, weights, cols, global_params, outer_moment, group_slot):
    rows, per_row = len(messages) + 1, len(blocks)
    size, width = blocks[0].shape
    depth = weights[0].shape[0]
    held = jax.ShapeDtypeStruct((global_params.shape[1] // LANES, LANES), jnp.float32)
    return pl.pallas_call(
        functools.partial(arrived_kernel, rows, cols, min(512, depth)),
        out_shape=[
            jax.ShapeDtypeStruct((size, depth), jnp.float32),
            jax.ShapeDtypeStruct((size, width), jnp.bfloat16),
            held,
            held,
            jax.ShapeDtypeStruct(own.shape, jnp.bfloat16),
        ],
        in_specs=[WHOLE] * (per_row + rows + cols - 1) + [pl.BlockSpec(memory_space=pltpu.SMEM), HBM, HBM],
        out_specs=[WHOLE] * 4 + [HBM],
        scratch_shapes=[
            pltpu.VMEM((cols, size, width), jnp.bfloat16),
            pltpu.VMEM(own.shape, jnp.bfloat16),
            pltpu.VMEM((global_params.size // LANES, LANES), jnp.float32),
            pltpu.VMEM((global_params.size // LANES, LANES), jnp.float32),
            pltpu.SemaphoreType.DMA,
            pltpu.SemaphoreType.DMA((2,)),
        ],
        compiler_params=params(24),
        cost_estimate=pl.CostEstimate(
            flops=2 * size * depth * width * (cols - 1), bytes_accessed=4 * size * depth, transcendentals=0
        ),
        name="arrived",
    )(
        *blocks, *messages, own, *weights, group_slot, in_hbm(interleaved(global_params)), in_hbm(interleaved(outer_moment))
    )


def finish_kernel(tile, sum_ref, block_ref, weight_ref, out_hbm, out_ref, sems):
    stores = []
    for i, start in enumerate(range(0, weight_ref.shape[0], tile)):
        features = pl.ds(start, tile)
        piece = times_transposed(block_ref[...], weight_ref[features, :])
        out_ref[:, features] = (sum_ref[:, features] + piece).astype(jnp.bfloat16)
        stores.append(pltpu.make_async_copy(out_ref.at[:, features], out_hbm.at[:, features], sems.at[i]))
        stores[-1].start()
    for store in stores:
        store.wait()


def finish(total, block, weight):
    size, depth = total.shape
    tile = min(512, depth)
    return pl.pallas_call(
        functools.partial(finish_kernel, tile),
        out_shape=jax.ShapeDtypeStruct((size, depth), jnp.bfloat16),
        in_specs=[WHOLE] * 3,
        out_specs=HBM,
        scratch_shapes=[pltpu.VMEM((size, depth), jnp.bfloat16), pltpu.SemaphoreType.DMA((depth // tile,))],
        compiler_params=params(16),
        cost_estimate=pl.CostEstimate(
            flops=2 * size * depth * block.shape[1], bytes_accessed=6 * size * depth, transcendentals=0
        ),
        name="finish",
    )(total, block, weight)


def merge_kernel(replicas, sum_ref, other_ref, held_ref, prior_ref, new_global_hbm, new_outer_hbm, *scratch):
    new_global_ref, new_outer_ref, sems = scratch
    average = (sum_ref[...].astype(jnp.float32) + other_ref[...].astype(jnp.float32)) / replicas
    new_outer = NESTEROV * prior_ref[...] + average
    new_outer_ref[...] = new_outer
    outer_store = pltpu.make_async_copy(new_outer_ref, new_outer_hbm, sems.at[0])
    outer_store.start()
    new_global_ref[...] = held_ref[...] - OUTER_RATE * (average + NESTEROV * new_outer)
    global_store = pltpu.make_async_copy(new_global_ref, new_global_hbm, sems.at[1])
    global_store.start()
    outer_store.wait()
    global_store.wait()


def interleaved(x):
    slots, size = x.shape
    return x.reshape(slots, size // LANES, LANES).transpose(1, 0, 2).reshape(slots * size // LANES, LANES)


def outer_sums(low, axis, early):
    n = lax.axis_size(axis)
    if not is_power_of_two(n):
        return lax.psum(low, axis), jnp.zeros_like(low)
    bit = 1
    while True:
        other = lax.ppermute(low, axis, swap_pairs(n, bit))
        bit *= 2
        if bit >= n:
            return low, other
        other, _ = after(other, early)
        low = (low.astype(jnp.float32) + other.astype(jnp.float32)).astype(jnp.bfloat16)


def merge(low, other, held, prior, replicas):
    shape = jax.ShapeDtypeStruct(low.shape, jnp.float32)
    new_global, new_outer = pl.pallas_call(
        functools.partial(merge_kernel, replicas),
        out_shape=[shape, shape],
        in_specs=[WHOLE] * 4,
        out_specs=[HBM] * 2,
        scratch_shapes=[pltpu.VMEM(low.shape, jnp.float32)] * 2 + [pltpu.SemaphoreType.DMA((2,))],
        compiler_params=params(16),
        cost_estimate=pl.CostEstimate(flops=8 * low.size, bytes_accessed=8 * low.size, transcendentals=0),
        name="merge",
    )(low, other, held, prior)
    return new_global.reshape(-1), new_outer.reshape(-1)


def on_device(
    tokens,
    cotangent,
    weight,
    first_moment,
    second_moment,
    outer_delta,
    global_params,
    outer_moment,
    group_slot,
):
    rows, cols = lax.axis_size("row"), lax.axis_size("col")
    replicas = lax.axis_size("rep")
    per_row = cols // rows
    cots = shifted(cotangent, "row")
    low_weight, low, chunks = prepare(weight[0], cotangent, outer_delta.reshape(-1, LANES), per_row)
    received = [lax.ppermute(chunks[k], ("row", "col"), chunk_pairs(rows, cols, per_row, k)) for k in range(per_row)]
    (new_weight, new_first, new_second), own, sends = inner(
        tokens, weight[0], first_moment[0], second_moment[0], cots, low_weight
    )
    weights = gather_offsets(low_weight, "col", sends)
    low, other = outer_sums(low, "rep", (sends, weights[1], weights[cols // 2]))
    received, _ = after(received, weights[cols // 2])
    messages = [lax.ppermute(m, "row", shift_pairs(rows, k + 1)) for k, m in enumerate(pack(received, sends))]
    total, block, held, prior, keys_values = arrived(
        received, messages, own, weights[:-1], cols, global_params, outer_moment, group_slot
    )
    new_global, new_outer = merge(low, other, held, prior, replicas)
    last, _ = after(weights[-1], (new_outer, total))
    input_grad = finish(total, block, last)
    return (keys_values, input_grad, new_weight[None], new_first[None], new_second[None], new_global, new_outer)


def solution(mesh):
    in_specs = (
        P("rep", "row"),
        P(("rep", "row"), "col"),
        P("rep", "row", "col"),
        P("rep", "row", "col"),
        P("rep", "row", "col"),
        P("rep", ("row", "col")),
        P(None, ("row", "col")),
        P(None, ("row", "col")),
        P(),
    )
    out_specs = (
        P(("rep", "row"), "col"),
        P(("rep", "col"), "row"),
        P("rep", "row", "col"),
        P("rep", "row", "col"),
        P("rep", "row", "col"),
        P(("row", "col")),
        P(("row", "col")),
    )
    return jax.shard_map(
        on_device, mesh=mesh, in_specs=in_specs, out_specs=out_specs, check_vma=False
    )
```

```python
import functools

import jax
import jax.numpy as jnp
from jax import lax
from jax.experimental import pallas as pl
from jax.experimental.pallas import tpu as pltpu
from jax.sharding import PartitionSpec as P

BETA_ONE = 0.9
BETA_TWO = 0.95
INNER_RATE = 0.0003
WEIGHT_DECAY = 0.1
EPSILON = 1e-08
OUTER_RATE = 0.7
NESTEROV = 0.9
LANES = 128
PARTS = 1

WHOLE = pl.BlockSpec(memory_space=pltpu.VMEM)
HBM = pl.BlockSpec(memory_space=pltpu.HBM)


def params(mebibytes):
    return pltpu.CompilerParams(vmem_limit_bytes=mebibytes * 1024 * 1024)


def after(x, others):
    return lax.optimization_barrier((x, others))


def in_hbm(x):
    return pltpu.with_memory_space_constraint(x, pltpu.HBM)


def is_power_of_two(n):
    return n & (n - 1) == 0


def swap_pairs(n, bit):
    return [(i, i ^ bit) for i in range(n)]


def shift_pairs(n, k):
    return [(i, (i + k) % n) for i in range(n)]


def mod(value, n):
    return lax.rem(value + n, n)


def gather_offsets(whole, parts, axis, early):
    n = lax.axis_size(axis)
    have = {0: [whole]}
    if is_power_of_two(n):
        bit = n // 2
        while bit:
            for k in list(have):
                sent = have[k] if k else parts if bit > 1 else [whole]
                if k:
                    sent, _ = after(sent, early)
                have[k ^ bit] = [lax.ppermute(part, axis, swap_pairs(n, bit)) for part in sent]
            bit //= 2
    else:
        for k in range(1, n):
            have[k] = [lax.ppermute(part, axis, shift_pairs(n, n - 1)) for part in have[k - 1]]
    return [have[k] for k in range(n)]


def owner_of(me, k, n):
    return me ^ k if is_power_of_two(n) else mod(me + k, n)


def shifted(block, axis):
    n = lax.axis_size(axis)
    return [block] + [lax.ppermute(block, axis, shift_pairs(n, k)) for k in range(1, n)]


def chunk_pairs(rows, cols, per_row, k):
    pairs = []
    for r in range(rows):
        for c in range(cols):
            pairs.append((r * cols + c, (c // per_row) * cols + r * per_row + (c + k) % per_row))
    return pairs


def round_kernel(pieces, source_hbm, *refs):
    whole_ref, part_refs, source_ref, sems = refs[0], refs[1:-2], refs[-2], refs[-1]
    size, part = source_ref.shape[0] // pieces, source_ref.shape[0] // len(part_refs)
    loads = []
    for i in range(pieces):
        some = pl.ds(i * size, size)
        loads.append(pltpu.make_async_copy(source_hbm.at[some, :], source_ref.at[some, :], sems.at[i]))
        loads[-1].start()
    for i in range(pieces):
        loads[i].wait()
        start = i * size
        low = source_ref[pl.ds(start, size), :].astype(jnp.bfloat16)
        whole_ref[pl.ds(start, size), :] = low
        part_refs[start // part][pl.ds(start % part, size), :] = low


def rounded(x, parts):
    pieces = 2 * parts
    shape = lambda rows: jax.ShapeDtypeStruct((rows, x.shape[1]), jnp.bfloat16)
    got = pl.pallas_call(
        functools.partial(round_kernel, pieces),
        out_shape=[shape(x.shape[0])] + [shape(x.shape[0] // parts)] * parts,
        in_specs=[HBM],
        out_specs=[WHOLE] * (1 + parts),
        scratch_shapes=[pltpu.VMEM(x.shape, jnp.float32), pltpu.SemaphoreType.DMA((pieces,))],
        compiler_params=params(16),
        cost_estimate=pl.CostEstimate(flops=0, bytes_accessed=8 * x.size, transcendentals=0),
        name="rounded",
    )(in_hbm(x))
    return got[0], got[1:]


def prepare_kernel(per_row, cot_hbm, delta_hbm, low_delta_ref, *refs):
    chunk_refs = refs[:per_row]
    delta_ref, sem, chunk_sems = refs[per_row:]
    size = chunk_refs[0].shape[0]
    col = lax.axis_index("col")
    load = pltpu.make_async_copy(delta_hbm, delta_ref, sem)
    load.start()
    chunks = []
    for k in range(per_row):
        start = pl.multiple_of(lax.rem(col + k, per_row) * size, size)
        chunks.append(pltpu.make_async_copy(cot_hbm.at[pl.ds(start, size), :], chunk_refs[k], chunk_sems.at[k]))
        chunks[-1].start()
    load.wait()
    low_delta_ref[...] = delta_ref[...].astype(jnp.bfloat16)
    for copy in chunks:
        copy.wait()


def prepare(cotangent, delta, per_row):
    chunk = cotangent.shape[0] // per_row
    shape = lambda *s: jax.ShapeDtypeStruct(s, jnp.bfloat16)
    outs = [shape(*delta.shape)] + [shape(chunk, cotangent.shape[1])] * per_row
    got = pl.pallas_call(
        functools.partial(prepare_kernel, per_row),
        out_shape=outs,
        in_specs=[HBM] * 2,
        out_specs=[WHOLE] * len(outs),
        scratch_shapes=[
            pltpu.VMEM(delta.shape, jnp.float32),
            pltpu.SemaphoreType.DMA,
            pltpu.SemaphoreType.DMA((per_row,)),
        ],
        compiler_params=params(16),
        cost_estimate=pl.CostEstimate(flops=0, bytes_accessed=6 * delta.size, transcendentals=0),
        name="prepare",
    )(*map(in_hbm, (cotangent, delta)))
    return got[0], got[1:]


def pack_kernel(*refs):
    size = refs[0].shape[0]
    for k, block_ref in enumerate(refs[:-1]):
        refs[-1][pl.ds(k * size, size), :] = block_ref[...]


def pack(blocks):
    size, width = blocks[0].shape
    return pl.pallas_call(
        pack_kernel,
        out_shape=jax.ShapeDtypeStruct((len(blocks) * size, width), jnp.bfloat16),
        in_specs=[WHOLE] * len(blocks),
        out_specs=WHOLE,
        compiler_params=params(16),
        cost_estimate=pl.CostEstimate(flops=0, bytes_accessed=4 * len(blocks) * size * width, transcendentals=0),
        name="pack",
    )(*blocks)


def inner_kernel(rows, steps, *refs):
    tokens_hbm, weight_hbm, first_hbm, second_hbm, cot_hbm, low_weight_ref = refs[:6]
    cot_refs = refs[6:5 + rows]
    new_weight_hbm, new_first_hbm, new_second_hbm, own_ref = refs[5 + rows:9 + rows]
    send_refs = refs[9 + rows:8 + 2 * rows]
    tokens_ref, state_ref, fresh_ref, cot_ref, total_ref, turned_ref, sems, out_sems, cot_sem = refs[-9:]
    row = lax.axis_index("row")
    part = cot_ref.shape[0]
    tile = tokens_ref.shape[1] // steps
    block = [pl.ds(s * tile, tile) for s in range(steps)]
    states = (weight_hbm, first_hbm, second_hbm)
    fresh = (new_weight_hbm, new_first_hbm, new_second_hbm)

    cot_load = pltpu.make_async_copy(cot_hbm, cot_ref, cot_sem)
    token_loads, state_loads, stores = [], [], []
    for s in range(steps):
        token_loads.append(pltpu.make_async_copy(tokens_hbm.at[:, block[s]], tokens_ref.at[:, block[s]], sems.at[s, 3]))
        state_loads.append([
            pltpu.make_async_copy(state.at[block[s], :], state_ref.at[i, block[s], :], sems.at[s, i])
            for i, state in enumerate(states)
        ])
        stores.append([
            pltpu.make_async_copy(fresh_ref.at[i, block[s], :], out.at[block[s], :], out_sems.at[s, i])
            for i, out in enumerate(fresh)
        ])
    cot_load.start()
    for s in range(steps):
        token_loads[s].start()
        for load in state_loads[s]:
            load.start()

    for k in range(1, rows):
        start = pl.multiple_of(mod(row - k, rows) * part, part)
        turned_ref[:, pl.ds(start, part)] = cot_refs[k - 1][...].T
    cot_load.wait()
    turned_ref[:, pl.ds(pl.multiple_of(row * part, part), part)] = cot_ref[...].T

    for s in range(steps):
        token_loads[s].wait()
        tokens = tokens_ref[:, block[s]]
        product = jnp.dot(tokens, low_weight_ref[block[s], :], preferred_element_type=jnp.float32)
        if s == 0:
            total_ref[...] = product
        else:
            total_ref[...] += product
        gradient = jnp.dot(turned_ref[...], tokens, preferred_element_type=jnp.float32).T
        for load in state_loads[s]:
            load.wait()
        weight = state_ref[0, block[s], :]
        first = BETA_ONE * state_ref[1, block[s], :] + (1.0 - BETA_ONE) * gradient
        second = BETA_TWO * state_ref[2, block[s], :] + (1.0 - BETA_TWO) * gradient * gradient
        fresh_ref[0, block[s], :] = weight - INNER_RATE * (
            first / (jnp.sqrt(second) + EPSILON) + WEIGHT_DECAY * weight
        )
        fresh_ref[1, block[s], :] = first
        fresh_ref[2, block[s], :] = second
        for store in stores[s]:
            store.start()

    own_ref[...] = total_ref[pl.ds(pl.multiple_of(row * part, part), part), :]
    for k in range(1, rows):
        start = pl.multiple_of(mod(row + k - rows, rows) * part, part)
        send_refs[k - 1][...] = total_ref[pl.ds(start, part), :].astype(jnp.bfloat16)
    for s in range(steps):
        for store in stores[s]:
            store.wait()


def inner(tokens, weight, first, second, cots, low_weight):
    rows = len(cots)
    count, depth = tokens.shape
    width = weight.shape[1]
    part = count // rows
    steps = depth // min(512, depth)
    full = jax.ShapeDtypeStruct((depth, width), jnp.float32)
    outs = [
        full,
        full,
        full,
        jax.ShapeDtypeStruct((part, width), jnp.float32),
    ] + [jax.ShapeDtypeStruct((part, width), jnp.bfloat16)] * (rows - 1)
    got = pl.pallas_call(
        functools.partial(inner_kernel, rows, steps),
        in_specs=[HBM] * 5 + [WHOLE] * rows,
        out_specs=[HBM] * 3 + [WHOLE] * rows,
        out_shape=outs,
        scratch_shapes=[
            pltpu.VMEM((count, depth), jnp.bfloat16),
            pltpu.VMEM((3, depth, width), jnp.float32),
            pltpu.VMEM((3, depth, width), jnp.float32),
            pltpu.VMEM((part, width), jnp.bfloat16),
            pltpu.VMEM((count, width), jnp.float32),
            pltpu.VMEM((width, count), jnp.bfloat16),
            pltpu.SemaphoreType.DMA((steps, 4)),
            pltpu.SemaphoreType.DMA((steps, 3)),
            pltpu.SemaphoreType.DMA,
        ],
        compiler_params=params(24),
        cost_estimate=pl.CostEstimate(
            flops=4 * count * depth * width, bytes_accessed=2 * count * depth + 24 * depth * width, transcendentals=0
        ),
        name="inner",
    )(*map(in_hbm, (tokens, weight, first, second, cots[0])), low_weight, *cots[1:])
    return got[:3], got[3], got[4:]


def times_transposed(left, right):
    return lax.dot_general(left, right, (((1,), (1,)), ((), ())), preferred_element_type=jnp.float32)


def arrived_kernel(rows, cols, counts, tile, *refs):
    per_row = cols // rows
    held_parts = sum(counts)
    block_refs, message_refs = refs[:per_row], refs[per_row:per_row + rows - 1]
    refs = refs[:per_row] + refs[per_row + rows - 1:]
    sum_refs = refs[per_row:per_row + rows - 1]
    own_ref = refs[per_row + rows - 1]
    part_refs = list(refs[per_row + rows:per_row + rows + held_parts])
    weight_refs = [[part_refs.pop(0) for _ in range(count)] for count in counts]
    slot_ref, global_hbm, moment_hbm, sum_ref, last_ref, held_ref, prior_ref, keys_values_hbm = refs[-14:-6]
    blocks_ref, keys_values_ref, global_ref, moment_ref, sem, slot_sems = refs[-6:]
    row, col = lax.axis_index("row"), lax.axis_index("col")
    loads = [
        pltpu.make_async_copy(global_hbm, global_ref, slot_sems.at[0]),
        pltpu.make_async_copy(moment_hbm, moment_ref, slot_sems.at[1]),
    ]
    for load in loads:
        load.start()
    size, part = block_refs[0].shape[0], own_ref.shape[0]
    total = own_ref[...]
    for other_ref in sum_refs:
        total += other_ref[...].astype(jnp.float32)
    keys_values_ref[...] = total.astype(jnp.bfloat16)
    store = pltpu.make_async_copy(keys_values_ref, keys_values_hbm, sem)
    store.start()
    for k in range(per_row):
        column = mod(lax.rem(col, per_row) - k, per_row)
        blocks_ref[row * per_row + column] = block_refs[k][...]
        for j in range(1, rows):
            blocks_ref[mod(row - j, rows) * per_row + column] = message_refs[j - 1][pl.ds(k * size, size), :]
    last_ref[...] = blocks_ref[owner_of(col, cols - 1, cols)]
    left = [blocks_ref[owner_of(col, k, cols)] for k in range(cols - 1)]
    for start in range(0, sum_ref.shape[1], tile):
        features = pl.ds(start, tile)
        tiles = []
        for parts in weight_refs:
            size = parts[0].shape[0]
            tiles.append(parts[start // size][pl.ds(start % size, tile), :])
        piece = None
        for k in range(0, cols - 1, 2):
            few = range(k, min(k + 2, cols - 1))
            product = times_transposed(
                jnp.concatenate([left[i] for i in few], axis=1),
                jnp.concatenate([tiles[i] for i in few], axis=1),
            )
            piece = product if piece is None else piece + product
        sum_ref[:, features] = piece
    slot, count = slot_ref[0], held_ref.shape[0]
    slots = global_ref.shape[0] // count
    for load, source_ref, out_ref in zip(loads, (global_ref, moment_ref), (held_ref, prior_ref)):
        load.wait()
        out_ref[...] = source_ref[pl.ds(slot, count, stride=slots), :]
    store.wait()


def arrived(blocks, messages, sums, own, weights, cols, global_params, outer_moment, group_slot):
    rows, per_row = len(messages) + 1, len(blocks)
    size, width = blocks[0].shape
    depth = sum(part.shape[0] for part in weights[0])
    parts = [part for block in weights for part in block]
    held = jax.ShapeDtypeStruct((global_params.shape[1] // LANES, LANES), jnp.float32)
    return pl.pallas_call(
        functools.partial(arrived_kernel, rows, cols, tuple(map(len, weights)), min(512, depth // PARTS)),
        out_shape=[
            jax.ShapeDtypeStruct((size, depth), jnp.float32),
            jax.ShapeDtypeStruct((size, width), jnp.bfloat16),
            held,
            held,
            jax.ShapeDtypeStruct(own.shape, jnp.bfloat16),
        ],
        in_specs=[WHOLE] * (per_row + 2 * rows - 1 + len(parts)) + [pl.BlockSpec(memory_space=pltpu.SMEM), HBM, HBM],
        out_specs=[WHOLE] * 4 + [HBM],
        scratch_shapes=[
            pltpu.VMEM((cols, size, width), jnp.bfloat16),
            pltpu.VMEM(own.shape, jnp.bfloat16),
            pltpu.VMEM((global_params.size // LANES, LANES), jnp.float32),
            pltpu.VMEM((global_params.size // LANES, LANES), jnp.float32),
            pltpu.SemaphoreType.DMA,
            pltpu.SemaphoreType.DMA((2,)),
        ],
        compiler_params=params(24),
        cost_estimate=pl.CostEstimate(
            flops=2 * size * depth * width * (cols - 1), bytes_accessed=4 * size * depth, transcendentals=0
        ),
        name="arrived",
    )(
        *blocks, *messages, *sums, own, *parts, group_slot, in_hbm(interleaved(global_params)), in_hbm(interleaved(outer_moment))
    )


def finish_kernel(tile, first, sum_ref, block_ref, weight_ref, *refs):
    out_hbm, out_ref, sems = refs[-3:]
    stores = []
    for i, start in enumerate(range(0, weight_ref.shape[0], tile)):
        features, target = pl.ds(start, tile), pl.ds(first + start, tile)
        piece = times_transposed(block_ref[...], weight_ref[features, :])
        out_ref[:, features] = (sum_ref[:, target] + piece).astype(jnp.bfloat16)
        stores.append(pltpu.make_async_copy(out_ref.at[:, features], out_hbm.at[:, target], sems.at[i]))
        stores[-1].start()
    for store in stores:
        store.wait()


def finish(total, block, weight, part, before):
    size, depth = total.shape
    count = weight.shape[0]
    tile = min(512, count)
    kept = [] if before is None else [before]
    return pl.pallas_call(
        functools.partial(finish_kernel, tile, part * count),
        out_shape=jax.ShapeDtypeStruct((size, depth), jnp.bfloat16),
        in_specs=[WHOLE] * 3 + [HBM] * len(kept),
        out_specs=HBM,
        scratch_shapes=[pltpu.VMEM((size, count), jnp.bfloat16), pltpu.SemaphoreType.DMA((count // tile,))],
        input_output_aliases={3: 0} if kept else {},
        compiler_params=params(16),
        cost_estimate=pl.CostEstimate(
            flops=2 * size * count * block.shape[1], bytes_accessed=6 * size * count, transcendentals=0
        ),
        name="finish",
    )(total, block, weight, *kept)


def merge_kernel(replicas, sum_ref, other_ref, held_ref, prior_ref, new_global_hbm, new_outer_hbm, *scratch):
    new_global_ref, new_outer_ref, sems = scratch
    average = (sum_ref[...].astype(jnp.float32) + other_ref[...].astype(jnp.float32)) / replicas
    new_outer = NESTEROV * prior_ref[...] + average
    new_outer_ref[...] = new_outer
    outer_store = pltpu.make_async_copy(new_outer_ref, new_outer_hbm, sems.at[0])
    outer_store.start()
    new_global_ref[...] = held_ref[...] - OUTER_RATE * (average + NESTEROV * new_outer)
    global_store = pltpu.make_async_copy(new_global_ref, new_global_hbm, sems.at[1])
    global_store.start()
    outer_store.wait()
    global_store.wait()


def interleaved(x):
    slots, size = x.shape
    return x.reshape(slots, size // LANES, LANES).transpose(1, 0, 2).reshape(slots * size // LANES, LANES)


def outer_sums(low, axis, early):
    n = lax.axis_size(axis)
    if not is_power_of_two(n):
        return lax.psum(low, axis), jnp.zeros_like(low)
    bit = 1
    while True:
        other = lax.ppermute(low, axis, swap_pairs(n, bit))
        bit *= 2
        if bit >= n:
            return low, other
        other, _ = after(other, early)
        low = (low.astype(jnp.float32) + other.astype(jnp.float32)).astype(jnp.bfloat16)


def merge(low, other, held, prior, replicas):
    shape = jax.ShapeDtypeStruct(low.shape, jnp.float32)
    new_global, new_outer = pl.pallas_call(
        functools.partial(merge_kernel, replicas),
        out_shape=[shape, shape],
        in_specs=[WHOLE] * 4,
        out_specs=[HBM] * 2,
        scratch_shapes=[pltpu.VMEM(low.shape, jnp.float32)] * 2 + [pltpu.SemaphoreType.DMA((2,))],
        compiler_params=params(16),
        cost_estimate=pl.CostEstimate(flops=8 * low.size, bytes_accessed=8 * low.size, transcendentals=0),
        name="merge",
    )(low, other, held, prior)
    return new_global.reshape(-1), new_outer.reshape(-1)


def on_device(
    tokens,
    cotangent,
    weight,
    first_moment,
    second_moment,
    outer_delta,
    global_params,
    outer_moment,
    group_slot,
):
    rows, cols = lax.axis_size("row"), lax.axis_size("col")
    replicas = lax.axis_size("rep")
    per_row = cols // rows
    cots = shifted(cotangent, "row")
    low_weight, low_parts = rounded(weight[0], PARTS)
    low, chunks = prepare(cotangent, outer_delta.reshape(-1, LANES), per_row)
    received = [lax.ppermute(chunks[k], ("row", "col"), chunk_pairs(rows, cols, per_row, k)) for k in range(per_row)]
    (new_weight, new_first, new_second), own, sends = inner(
        tokens, weight[0], first_moment[0], second_moment[0], cots, low_weight
    )
    weights = gather_offsets(low_weight, low_parts, "col", sends)
    low, other = outer_sums(low, "rep", (sends, weights[1], weights[cols // 2]))
    received, _ = after(received, weights[cols // 2])
    sums = [lax.ppermute(m, "row", shift_pairs(rows, k + 1)) for k, m in enumerate(sends)]
    messages = [lax.ppermute(pack(received), "row", shift_pairs(rows, k)) for k in range(1, rows)]
    total, block, held, prior, keys_values = arrived(
        received, messages, sums, own, weights[:-1], cols, global_params, outer_moment, group_slot
    )
    new_global, new_outer = merge(low, other, held, prior, replicas)
    input_grad = None
    for part, last in enumerate(weights[-1]):
        last, _ = after(last, total if input_grad is None else (new_outer, input_grad))
        input_grad = finish(total, block, last, part, input_grad)
    return (keys_values, input_grad, new_weight[None], new_first[None], new_second[None], new_global, new_outer)


def solution(mesh):
    in_specs = (
        P("rep", "row"),
        P(("rep", "row"), "col"),
        P("rep", "row", "col"),
        P("rep", "row", "col"),
        P("rep", "row", "col"),
        P("rep", ("row", "col")),
        P(None, ("row", "col")),
        P(None, ("row", "col")),
        P(),
    )
    out_specs = (
        P(("rep", "row"), "col"),
        P(("rep", "col"), "row"),
        P("rep", "row", "col"),
        P("rep", "row", "col"),
        P("rep", "row", "col"),
        P(("row", "col")),
        P(("row", "col")),
    )
    return jax.shard_map(
        on_device, mesh=mesh, in_specs=in_specs, out_specs=out_specs, check_vma=False
    )
```

```python
import functools

import jax
import jax.numpy as jnp
from jax import lax
from jax.experimental import pallas as pl
from jax.experimental.pallas import tpu as pltpu
from jax.sharding import PartitionSpec as P

BETA_ONE = 0.9
BETA_TWO = 0.95
INNER_RATE = 0.0003
WEIGHT_DECAY = 0.1
EPSILON = 1e-08
OUTER_RATE = 0.7
NESTEROV = 0.9
LANES = 128

WHOLE = pl.BlockSpec(memory_space=pltpu.VMEM)
HBM = pl.BlockSpec(memory_space=pltpu.HBM)


def params(mebibytes):
    return pltpu.CompilerParams(vmem_limit_bytes=mebibytes * 1024 * 1024)


def after(x, others):
    return lax.optimization_barrier((x, others))


def in_hbm(x):
    return pltpu.with_memory_space_constraint(x, pltpu.HBM)


def is_power_of_two(n):
    return n & (n - 1) == 0


def swap_pairs(n, bit):
    return [(i, i ^ bit) for i in range(n)]


def shift_pairs(n, k):
    return [(i, (i + k) % n) for i in range(n)]


def mod(value, n):
    return lax.rem(value + n, n)


def gather_offsets(block, axis, early):
    n = lax.axis_size(axis)
    have = {0: block}
    if is_power_of_two(n):
        bit = n // 2
        while bit:
            for k in list(have):
                if k:
                    have[k], _ = after(have[k], early)
                have[k ^ bit] = lax.ppermute(have[k], axis, swap_pairs(n, bit))
            bit //= 2
    else:
        for k in range(1, n):
            have[k] = lax.ppermute(have[k - 1], axis, shift_pairs(n, n - 1))
    return [have[k] for k in range(n)]


def owner_of(me, k, n):
    return me ^ k if is_power_of_two(n) else mod(me + k, n)


def shifted(block, axis):
    n = lax.axis_size(axis)
    return [block] + [lax.ppermute(block, axis, shift_pairs(n, k)) for k in range(1, n)]


def chunk_pairs(rows, cols, per_row, k):
    pairs = []
    for r in range(rows):
        for c in range(cols):
            pairs.append((r * cols + c, (c // per_row) * cols + r * per_row + (c + k) % per_row))
    return pairs


def round_kernel(pieces, source_hbm, out_ref, source_ref, sems):
    size = source_ref.shape[0] // pieces
    parts = [pl.ds(i * size, size) for i in range(pieces)]
    loads = [pltpu.make_async_copy(source_hbm.at[p, :], source_ref.at[p, :], sems.at[i]) for i, p in enumerate(parts)]
    for load in loads:
        load.start()
    for load, part in zip(loads, parts):
        load.wait()
        out_ref[part, :] = source_ref[part, :].astype(jnp.bfloat16)


def rounded(x):
    pieces = 2
    return pl.pallas_call(
        functools.partial(round_kernel, pieces),
        out_shape=jax.ShapeDtypeStruct(x.shape, jnp.bfloat16),
        in_specs=[HBM],
        out_specs=WHOLE,
        scratch_shapes=[pltpu.VMEM(x.shape, jnp.float32), pltpu.SemaphoreType.DMA((pieces,))],
        compiler_params=params(16),
        cost_estimate=pl.CostEstimate(flops=0, bytes_accessed=6 * x.size, transcendentals=0),
        name="rounded",
    )(in_hbm(x))


def prepare_kernel(per_row, cot_hbm, delta_hbm, low_delta_ref, *refs):
    chunk_refs = refs[:per_row]
    delta_ref, sem, chunk_sems = refs[per_row:]
    size = chunk_refs[0].shape[0]
    col = lax.axis_index("col")
    load = pltpu.make_async_copy(delta_hbm, delta_ref, sem)
    load.start()
    chunks = []
    for k in range(per_row):
        start = pl.multiple_of(lax.rem(col + k, per_row) * size, size)
        chunks.append(pltpu.make_async_copy(cot_hbm.at[pl.ds(start, size), :], chunk_refs[k], chunk_sems.at[k]))
        chunks[-1].start()
    load.wait()
    low_delta_ref[...] = delta_ref[...].astype(jnp.bfloat16)
    for copy in chunks:
        copy.wait()


def prepare(cotangent, delta, per_row):
    chunk = cotangent.shape[0] // per_row
    shape = lambda *s: jax.ShapeDtypeStruct(s, jnp.bfloat16)
    outs = [shape(*delta.shape)] + [shape(chunk, cotangent.shape[1])] * per_row
    got = pl.pallas_call(
        functools.partial(prepare_kernel, per_row),
        out_shape=outs,
        in_specs=[HBM] * 2,
        out_specs=[WHOLE] * len(outs),
        scratch_shapes=[
            pltpu.VMEM(delta.shape, jnp.float32),
            pltpu.SemaphoreType.DMA,
            pltpu.SemaphoreType.DMA((per_row,)),
        ],
        compiler_params=params(16),
        cost_estimate=pl.CostEstimate(flops=0, bytes_accessed=6 * delta.size, transcendentals=0),
        name="prepare",
    )(*map(in_hbm, (cotangent, delta)))
    return got[0], got[1:]


def pack_kernel(*refs):
    size = refs[0].shape[0]
    for k, block_ref in enumerate(refs[:-1]):
        refs[-1][pl.ds(k * size, size), :] = block_ref[...]


def pack(blocks):
    size, width = blocks[0].shape
    return pl.pallas_call(
        pack_kernel,
        out_shape=jax.ShapeDtypeStruct((len(blocks) * size, width), jnp.bfloat16),
        in_specs=[WHOLE] * len(blocks),
        out_specs=WHOLE,
        compiler_params=params(16),
        cost_estimate=pl.CostEstimate(flops=0, bytes_accessed=4 * len(blocks) * size * width, transcendentals=0),
        name="pack",
    )(*blocks)


def inner_kernel(rows, steps, *refs):
    tokens_hbm, weight_hbm, first_hbm, second_hbm, cot_hbm, low_weight_ref = refs[:6]
    cot_refs = refs[6:5 + rows]
    new_weight_hbm, new_first_hbm, new_second_hbm, own_ref = refs[5 + rows:9 + rows]
    send_refs = refs[9 + rows:8 + 2 * rows]
    tokens_ref, state_ref, fresh_ref, cot_ref, total_ref, turned_ref, sems, out_sems, cot_sem = refs[-9:]
    row = lax.axis_index("row")
    part = cot_ref.shape[0]
    tile = tokens_ref.shape[1] // steps
    block = [pl.ds(s * tile, tile) for s in range(steps)]
    states = (weight_hbm, first_hbm, second_hbm)
    fresh = (new_weight_hbm, new_first_hbm, new_second_hbm)

    cot_load = pltpu.make_async_copy(cot_hbm, cot_ref, cot_sem)
    token_loads, state_loads, stores = [], [], []
    for s in range(steps):
        token_loads.append(pltpu.make_async_copy(tokens_hbm.at[:, block[s]], tokens_ref.at[:, block[s]], sems.at[s, 3]))
        state_loads.append([
            pltpu.make_async_copy(state.at[block[s], :], state_ref.at[i, block[s], :], sems.at[s, i])
            for i, state in enumerate(states)
        ])
        stores.append([
            pltpu.make_async_copy(fresh_ref.at[i, block[s], :], out.at[block[s], :], out_sems.at[s, i])
            for i, out in enumerate(fresh)
        ])
    cot_load.start()
    for s in range(steps):
        token_loads[s].start()
        for load in state_loads[s]:
            load.start()

    for k in range(1, rows):
        start = pl.multiple_of(mod(row - k, rows) * part, part)
        turned_ref[:, pl.ds(start, part)] = cot_refs[k - 1][...].T
    cot_load.wait()
    turned_ref[:, pl.ds(pl.multiple_of(row * part, part), part)] = cot_ref[...].T

    for s in range(steps):
        token_loads[s].wait()
        tokens = tokens_ref[:, block[s]]
        product = jnp.dot(tokens, low_weight_ref[block[s], :], preferred_element_type=jnp.float32)
        if s == 0:
            total_ref[...] = product
        else:
            total_ref[...] += product
        gradient = jnp.dot(turned_ref[...], tokens, preferred_element_type=jnp.float32).T
        for load in state_loads[s]:
            load.wait()
        weight = state_ref[0, block[s], :]
        first = BETA_ONE * state_ref[1, block[s], :] + (1.0 - BETA_ONE) * gradient
        second = BETA_TWO * state_ref[2, block[s], :] + (1.0 - BETA_TWO) * gradient * gradient
        fresh_ref[0, block[s], :] = weight - INNER_RATE * (
            first / (jnp.sqrt(second) + EPSILON) + WEIGHT_DECAY * weight
        )
        fresh_ref[1, block[s], :] = first
        fresh_ref[2, block[s], :] = second
        for store in stores[s]:
            store.start()

    own_ref[...] = total_ref[pl.ds(pl.multiple_of(row * part, part), part), :]
    for k in range(1, rows):
        start = pl.multiple_of(mod(row + k - rows, rows) * part, part)
        send_refs[k - 1][...] = total_ref[pl.ds(start, part), :].astype(jnp.bfloat16)
    for s in range(steps):
        for store in stores[s]:
            store.wait()


def inner(tokens, weight, first, second, cots, low_weight):
    rows = len(cots)
    count, depth = tokens.shape
    width = weight.shape[1]
    part = count // rows
    steps = depth // min(512, depth)
    full = jax.ShapeDtypeStruct((depth, width), jnp.float32)
    outs = [
        full,
        full,
        full,
        jax.ShapeDtypeStruct((part, width), jnp.float32),
    ] + [jax.ShapeDtypeStruct((part, width), jnp.bfloat16)] * (rows - 1)
    got = pl.pallas_call(
        functools.partial(inner_kernel, rows, steps),
        in_specs=[HBM] * 5 + [WHOLE] * rows,
        out_specs=[HBM] * 3 + [WHOLE] * rows,
        out_shape=outs,
        scratch_shapes=[
            pltpu.VMEM((count, depth), jnp.bfloat16),
            pltpu.VMEM((3, depth, width), jnp.float32),
            pltpu.VMEM((3, depth, width), jnp.float32),
            pltpu.VMEM((part, width), jnp.bfloat16),
            pltpu.VMEM((count, width), jnp.float32),
            pltpu.VMEM((width, count), jnp.bfloat16),
            pltpu.SemaphoreType.DMA((steps, 4)),
            pltpu.SemaphoreType.DMA((steps, 3)),
            pltpu.SemaphoreType.DMA,
        ],
        compiler_params=params(24),
        cost_estimate=pl.CostEstimate(
            flops=4 * count * depth * width, bytes_accessed=2 * count * depth + 24 * depth * width, transcendentals=0
        ),
        name="inner",
    )(*map(in_hbm, (tokens, weight, first, second, cots[0])), low_weight, *cots[1:])
    return got[:3], got[3], got[4:]


def times_transposed(left, right):
    return lax.dot_general(left, right, (((1,), (1,)), ((), ())), preferred_element_type=jnp.float32)


def arrived_kernel(rows, cols, tile, *refs):
    per_row = cols // rows
    block_refs, message_refs = refs[:per_row], refs[per_row:per_row + rows - 1]
    refs = refs[:per_row] + refs[per_row + rows - 1:]
    sum_refs = refs[per_row:per_row + rows - 1]
    own_ref = refs[per_row + rows - 1]
    weight_refs = refs[per_row + rows:per_row + rows + cols - 1]
    slot_ref, global_hbm, moment_hbm, sum_ref, last_ref, held_ref, prior_ref, keys_values_hbm = refs[-14:-6]
    blocks_ref, keys_values_ref, global_ref, moment_ref, sem, slot_sems = refs[-6:]
    row, col = lax.axis_index("row"), lax.axis_index("col")
    loads = [
        pltpu.make_async_copy(global_hbm, global_ref, slot_sems.at[0]),
        pltpu.make_async_copy(moment_hbm, moment_ref, slot_sems.at[1]),
    ]
    for load in loads:
        load.start()
    size, part = block_refs[0].shape[0], own_ref.shape[0]
    total = own_ref[...]
    for other_ref in sum_refs:
        total += other_ref[...].astype(jnp.float32)
    keys_values_ref[...] = total.astype(jnp.bfloat16)
    store = pltpu.make_async_copy(keys_values_ref, keys_values_hbm, sem)
    store.start()
    for k in range(per_row):
        column = mod(lax.rem(col, per_row) - k, per_row)
        blocks_ref[row * per_row + column] = block_refs[k][...]
        for j in range(1, rows):
            blocks_ref[mod(row - j, rows) * per_row + column] = message_refs[j - 1][pl.ds(k * size, size), :]
    last_ref[...] = blocks_ref[owner_of(col, cols - 1, cols)]
    left = [blocks_ref[owner_of(col, k, cols)] for k in range(cols - 1)]
    for start in range(0, weight_refs[0].shape[0], tile):
        features = pl.ds(start, tile)
        piece = None
        for k in range(0, cols - 1, 2):
            few = range(k, min(k + 2, cols - 1))
            product = times_transposed(
                jnp.concatenate([left[i] for i in few], axis=1),
                jnp.concatenate([weight_refs[i][features, :] for i in few], axis=1),
            )
            piece = product if piece is None else piece + product
        sum_ref[:, features] = piece
    slot, count = slot_ref[0], held_ref.shape[0]
    slots = global_ref.shape[0] // count
    for load, source_ref, out_ref in zip(loads, (global_ref, moment_ref), (held_ref, prior_ref)):
        load.wait()
        out_ref[...] = source_ref[pl.ds(slot, count, stride=slots), :]
    store.wait()


def arrived(blocks, messages, sums, own, weights, cols, global_params, outer_moment, group_slot):
    rows, per_row = len(messages) + 1, len(blocks)
    size, width = blocks[0].shape
    depth = weights[0].shape[0]
    held = jax.ShapeDtypeStruct((global_params.shape[1] // LANES, LANES), jnp.float32)
    return pl.pallas_call(
        functools.partial(arrived_kernel, rows, cols, min(512, depth)),
        out_shape=[
            jax.ShapeDtypeStruct((size, depth), jnp.float32),
            jax.ShapeDtypeStruct((size, width), jnp.bfloat16),
            held,
            held,
            jax.ShapeDtypeStruct(own.shape, jnp.bfloat16),
        ],
        in_specs=[WHOLE] * (per_row + 2 * rows - 1 + cols - 1) + [pl.BlockSpec(memory_space=pltpu.SMEM), HBM, HBM],
        out_specs=[WHOLE] * 4 + [HBM],
        scratch_shapes=[
            pltpu.VMEM((cols, size, width), jnp.bfloat16),
            pltpu.VMEM(own.shape, jnp.bfloat16),
            pltpu.VMEM((global_params.size // LANES, LANES), jnp.float32),
            pltpu.VMEM((global_params.size // LANES, LANES), jnp.float32),
            pltpu.SemaphoreType.DMA,
            pltpu.SemaphoreType.DMA((2,)),
        ],
        compiler_params=params(24),
        cost_estimate=pl.CostEstimate(
            flops=2 * size * depth * width * (cols - 1), bytes_accessed=4 * size * depth, transcendentals=0
        ),
        name="arrived",
    )(
        *blocks, *messages, *sums, own, *weights, group_slot, in_hbm(interleaved(global_params)), in_hbm(interleaved(outer_moment))
    )


def finish_kernel(tile, sum_ref, block_ref, weight_ref, out_hbm, out_ref, sems):
    stores = []
    for i, start in enumerate(range(0, weight_ref.shape[0], tile)):
        features = pl.ds(start, tile)
        piece = times_transposed(block_ref[...], weight_ref[features, :])
        out_ref[:, features] = (sum_ref[:, features] + piece).astype(jnp.bfloat16)
        stores.append(pltpu.make_async_copy(out_ref.at[:, features], out_hbm.at[:, features], sems.at[i]))
        stores[-1].start()
    for store in stores:
        store.wait()


def finish(total, block, weight):
    size, depth = total.shape
    tile = min(512, depth)
    return pl.pallas_call(
        functools.partial(finish_kernel, tile),
        out_shape=jax.ShapeDtypeStruct((size, depth), jnp.bfloat16),
        in_specs=[WHOLE] * 3,
        out_specs=HBM,
        scratch_shapes=[pltpu.VMEM((size, depth), jnp.bfloat16), pltpu.SemaphoreType.DMA((depth // tile,))],
        compiler_params=params(16),
        cost_estimate=pl.CostEstimate(
            flops=2 * size * depth * block.shape[1], bytes_accessed=6 * size * depth, transcendentals=0
        ),
        name="finish",
    )(total, block, weight)


def merge_kernel(replicas, sum_ref, other_ref, held_ref, prior_ref, new_global_hbm, new_outer_hbm, *scratch):
    new_global_ref, new_outer_ref, sems = scratch
    average = (sum_ref[...].astype(jnp.float32) + other_ref[...].astype(jnp.float32)) / replicas
    new_outer = NESTEROV * prior_ref[...] + average
    new_outer_ref[...] = new_outer
    outer_store = pltpu.make_async_copy(new_outer_ref, new_outer_hbm, sems.at[0])
    outer_store.start()
    new_global_ref[...] = held_ref[...] - OUTER_RATE * (average + NESTEROV * new_outer)
    global_store = pltpu.make_async_copy(new_global_ref, new_global_hbm, sems.at[1])
    global_store.start()
    outer_store.wait()
    global_store.wait()


def interleaved(x):
    slots, size = x.shape
    return x.reshape(slots, size // LANES, LANES).transpose(1, 0, 2).reshape(slots * size // LANES, LANES)


def outer_sums(low, axis, early):
    n = lax.axis_size(axis)
    if not is_power_of_two(n):
        return lax.psum(low, axis), jnp.zeros_like(low)
    bit = 1
    while True:
        other = lax.ppermute(low, axis, swap_pairs(n, bit))
        bit *= 2
        if bit >= n:
            return low, other
        other, _ = after(other, early)
        low = (low.astype(jnp.float32) + other.astype(jnp.float32)).astype(jnp.bfloat16)


def merge(low, other, held, prior, replicas):
    shape = jax.ShapeDtypeStruct(low.shape, jnp.float32)
    new_global, new_outer = pl.pallas_call(
        functools.partial(merge_kernel, replicas),
        out_shape=[shape, shape],
        in_specs=[WHOLE] * 4,
        out_specs=[HBM] * 2,
        scratch_shapes=[pltpu.VMEM(low.shape, jnp.float32)] * 2 + [pltpu.SemaphoreType.DMA((2,))],
        compiler_params=params(16),
        cost_estimate=pl.CostEstimate(flops=8 * low.size, bytes_accessed=8 * low.size, transcendentals=0),
        name="merge",
    )(low, other, held, prior)
    return new_global.reshape(-1), new_outer.reshape(-1)


def on_device(
    tokens,
    cotangent,
    weight,
    first_moment,
    second_moment,
    outer_delta,
    global_params,
    outer_moment,
    group_slot,
):
    rows, cols = lax.axis_size("row"), lax.axis_size("col")
    replicas = lax.axis_size("rep")
    per_row = cols // rows
    cots = shifted(cotangent, "row")
    low_weight = rounded(weight[0])
    low, chunks = prepare(cotangent, outer_delta.reshape(-1, LANES), per_row)
    received = [lax.ppermute(chunks[k], ("row", "col"), chunk_pairs(rows, cols, per_row, k)) for k in range(per_row)]
    (new_weight, new_first, new_second), own, sends = inner(
        tokens, weight[0], first_moment[0], second_moment[0], cots, low_weight
    )
    weights = gather_offsets(low_weight, "col", sends)
    low, other = outer_sums(low, "rep", (sends, weights[1], weights[cols // 2]))
    received, _ = after(received, weights[cols // 2])
    sums = [lax.ppermute(m, "row", shift_pairs(rows, k + 1)) for k, m in enumerate(sends)]
    messages = [lax.ppermute(pack(received), "row", shift_pairs(rows, k)) for k in range(1, rows)]
    total, block, held, prior, keys_values = arrived(
        received, messages, sums, own, weights[:-1], cols, global_params, outer_moment, group_slot
    )
    new_global, new_outer = merge(low, other, held, prior, replicas)
    last, _ = after(weights[-1], (new_outer, total))
    input_grad = finish(total, block, last)
    return (keys_values, input_grad, new_weight[None], new_first[None], new_second[None], new_global, new_outer)


def solution(mesh):
    in_specs = (
        P("rep", "row"),
        P(("rep", "row"), "col"),
        P("rep", "row", "col"),
        P("rep", "row", "col"),
        P("rep", "row", "col"),
        P("rep", ("row", "col")),
        P(None, ("row", "col")),
        P(None, ("row", "col")),
        P(),
    )
    out_specs = (
        P(("rep", "row"), "col"),
        P(("rep", "col"), "row"),
        P("rep", "row", "col"),
        P("rep", "row", "col"),
        P("rep", "row", "col"),
        P(("row", "col")),
        P(("row", "col")),
    )
    return jax.shard_map(
        on_device, mesh=mesh, in_specs=in_specs, out_specs=out_specs, check_vma=False
    )
```

```python
import functools

import jax
import jax.numpy as jnp
from jax import lax
from jax.experimental import pallas as pl
from jax.experimental.pallas import tpu as pltpu
from jax.sharding import PartitionSpec as P

BETA_ONE = 0.9
BETA_TWO = 0.95
INNER_RATE = 0.0003
WEIGHT_DECAY = 0.1
EPSILON = 1e-08
OUTER_RATE = 0.7
NESTEROV = 0.9
LANES = 128

WHOLE = pl.BlockSpec(memory_space=pltpu.VMEM)
HBM = pl.BlockSpec(memory_space=pltpu.HBM)


def params(mebibytes):
    return pltpu.CompilerParams(vmem_limit_bytes=mebibytes * 1024 * 1024)


def after(x, others):
    return lax.optimization_barrier((x, others))


def in_hbm(x):
    return pltpu.with_memory_space_constraint(x, pltpu.HBM)


def is_power_of_two(n):
    return n & (n - 1) == 0


def swap_pairs(n, bit):
    return [(i, i ^ bit) for i in range(n)]


def shift_pairs(n, k):
    return [(i, (i + k) % n) for i in range(n)]


def mod(value, n):
    return lax.rem(value + n, n)


def gather_offsets(block, axis, early):
    n = lax.axis_size(axis)
    have = {0: block}
    if is_power_of_two(n):
        bit = n // 2
        while bit:
            for k in list(have):
                if k:
                    have[k], _ = after(have[k], early)
                have[k ^ bit] = lax.ppermute(have[k], axis, swap_pairs(n, bit))
            bit //= 2
    else:
        for k in range(1, n):
            have[k] = lax.ppermute(have[k - 1], axis, shift_pairs(n, n - 1))
    return [have[k] for k in range(n)]


def owner_of(me, k, n):
    return me ^ k if is_power_of_two(n) else mod(me + k, n)


def shifted(block, axis):
    n = lax.axis_size(axis)
    return [block] + [lax.ppermute(block, axis, shift_pairs(n, k)) for k in range(1, n)]


def chunk_pairs(rows, cols, per_row, k):
    pairs = []
    for r in range(rows):
        for c in range(cols):
            pairs.append((r * cols + c, (c // per_row) * cols + r * per_row + (c + k) % per_row))
    return pairs


def round_kernel(pieces, source_hbm, out_ref, source_ref, sems):
    size = source_ref.shape[0] // pieces
    parts = [pl.ds(i * size, size) for i in range(pieces)]
    loads = [pltpu.make_async_copy(source_hbm.at[p, :], source_ref.at[p, :], sems.at[i]) for i, p in enumerate(parts)]
    for load in loads:
        load.start()
    for load, part in zip(loads, parts):
        load.wait()
        out_ref[part, :] = source_ref[part, :].astype(jnp.bfloat16)


def rounded(x):
    pieces = 2
    return pl.pallas_call(
        functools.partial(round_kernel, pieces),
        out_shape=jax.ShapeDtypeStruct(x.shape, jnp.bfloat16),
        in_specs=[HBM],
        out_specs=WHOLE,
        scratch_shapes=[pltpu.VMEM(x.shape, jnp.float32), pltpu.SemaphoreType.DMA((pieces,))],
        compiler_params=params(16),
        cost_estimate=pl.CostEstimate(flops=0, bytes_accessed=6 * x.size, transcendentals=0),
        name="rounded",
    )(in_hbm(x))


def prepare_kernel(per_row, cot_hbm, delta_hbm, low_delta_ref, *refs):
    chunk_refs = refs[:per_row]
    delta_ref, sem, chunk_sems = refs[per_row:]
    size = chunk_refs[0].shape[0]
    col = lax.axis_index("col")
    load = pltpu.make_async_copy(delta_hbm, delta_ref, sem)
    load.start()
    chunks = []
    for k in range(per_row):
        start = pl.multiple_of(lax.rem(col + k, per_row) * size, size)
        chunks.append(pltpu.make_async_copy(cot_hbm.at[pl.ds(start, size), :], chunk_refs[k], chunk_sems.at[k]))
        chunks[-1].start()
    load.wait()
    low_delta_ref[...] = delta_ref[...].astype(jnp.bfloat16)
    for copy in chunks:
        copy.wait()


def prepare(cotangent, delta, per_row):
    chunk = cotangent.shape[0] // per_row
    shape = lambda *s: jax.ShapeDtypeStruct(s, jnp.bfloat16)
    outs = [shape(*delta.shape)] + [shape(chunk, cotangent.shape[1])] * per_row
    got = pl.pallas_call(
        functools.partial(prepare_kernel, per_row),
        out_shape=outs,
        in_specs=[HBM] * 2,
        out_specs=[WHOLE] * len(outs),
        scratch_shapes=[
            pltpu.VMEM(delta.shape, jnp.float32),
            pltpu.SemaphoreType.DMA,
            pltpu.SemaphoreType.DMA((per_row,)),
        ],
        compiler_params=params(16),
        cost_estimate=pl.CostEstimate(flops=0, bytes_accessed=6 * delta.size, transcendentals=0),
        name="prepare",
    )(*map(in_hbm, (cotangent, delta)))
    return got[0], got[1:]


def pack_kernel(*refs):
    size = refs[0].shape[0]
    for k, block_ref in enumerate(refs[:-1]):
        refs[-1][pl.ds(k * size, size), :] = block_ref[...]


def pack(blocks):
    size, width = blocks[0].shape
    return pl.pallas_call(
        pack_kernel,
        out_shape=jax.ShapeDtypeStruct((len(blocks) * size, width), jnp.bfloat16),
        in_specs=[WHOLE] * len(blocks),
        out_specs=WHOLE,
        compiler_params=params(16),
        cost_estimate=pl.CostEstimate(flops=0, bytes_accessed=4 * len(blocks) * size * width, transcendentals=0),
        name="pack",
    )(*blocks)


def inner_kernel(rows, steps, *refs):
    tokens_hbm, weight_hbm, first_hbm, second_hbm, cot_hbm, low_weight_ref = refs[:6]
    cot_refs = refs[6:5 + rows]
    new_weight_hbm, new_first_hbm, new_second_hbm, own_ref = refs[5 + rows:9 + rows]
    send_refs = refs[9 + rows:8 + 2 * rows]
    tokens_ref, state_ref, fresh_ref, cot_ref, total_ref, turned_ref, sems, out_sems, cot_sem = refs[-9:]
    row = lax.axis_index("row")
    part = cot_ref.shape[0]
    tile = tokens_ref.shape[1] // steps
    block = [pl.ds(s * tile, tile) for s in range(steps)]
    states = (weight_hbm, first_hbm, second_hbm)
    fresh = (new_weight_hbm, new_first_hbm, new_second_hbm)

    cot_load = pltpu.make_async_copy(cot_hbm, cot_ref, cot_sem)
    token_loads, state_loads, stores = [], [], []
    for s in range(steps):
        token_loads.append(pltpu.make_async_copy(tokens_hbm.at[:, block[s]], tokens_ref.at[:, block[s]], sems.at[s, 3]))
        state_loads.append([
            pltpu.make_async_copy(state.at[block[s], :], state_ref.at[i, block[s], :], sems.at[s, i])
            for i, state in enumerate(states)
        ])
        stores.append([
            pltpu.make_async_copy(fresh_ref.at[i, block[s], :], out.at[block[s], :], out_sems.at[s, i])
            for i, out in enumerate(fresh)
        ])
    cot_load.start()
    for s in range(steps):
        token_loads[s].start()
        for load in state_loads[s]:
            load.start()

    for k in range(1, rows):
        start = pl.multiple_of(mod(row - k, rows) * part, part)
        turned_ref[:, pl.ds(start, part)] = cot_refs[k - 1][...].T
    cot_load.wait()
    turned_ref[:, pl.ds(pl.multiple_of(row * part, part), part)] = cot_ref[...].T

    for s in range(steps):
        token_loads[s].wait()
        tokens = tokens_ref[:, block[s]]
        product = jnp.dot(tokens, low_weight_ref[block[s], :], preferred_element_type=jnp.float32)
        if s == 0:
            total_ref[...] = product
        else:
            total_ref[...] += product
        gradient = jnp.dot(turned_ref[...], tokens, preferred_element_type=jnp.float32).T
        for load in state_loads[s]:
            load.wait()
        weight = state_ref[0, block[s], :]
        first = BETA_ONE * state_ref[1, block[s], :] + (1.0 - BETA_ONE) * gradient
        second = BETA_TWO * state_ref[2, block[s], :] + (1.0 - BETA_TWO) * gradient * gradient
        fresh_ref[0, block[s], :] = weight - INNER_RATE * (
            first / (jnp.sqrt(second) + EPSILON) + WEIGHT_DECAY * weight
        )
        fresh_ref[1, block[s], :] = first
        fresh_ref[2, block[s], :] = second
        for store in stores[s]:
            store.start()

    own_ref[...] = total_ref[pl.ds(pl.multiple_of(row * part, part), part), :]
    for k in range(1, rows):
        start = pl.multiple_of(mod(row + k - rows, rows) * part, part)
        send_refs[k - 1][...] = total_ref[pl.ds(start, part), :].astype(jnp.bfloat16)
    for s in range(steps):
        for store in stores[s]:
            store.wait()


def inner(tokens, weight, first, second, cots, low_weight):
    rows = len(cots)
    count, depth = tokens.shape
    width = weight.shape[1]
    part = count // rows
    steps = depth // min(512, depth)
    full = jax.ShapeDtypeStruct((depth, width), jnp.float32)
    outs = [
        full,
        full,
        full,
        jax.ShapeDtypeStruct((part, width), jnp.float32),
    ] + [jax.ShapeDtypeStruct((part, width), jnp.bfloat16)] * (rows - 1)
    got = pl.pallas_call(
        functools.partial(inner_kernel, rows, steps),
        in_specs=[HBM] * 5 + [WHOLE] * rows,
        out_specs=[HBM] * 3 + [WHOLE] * rows,
        out_shape=outs,
        scratch_shapes=[
            pltpu.VMEM((count, depth), jnp.bfloat16),
            pltpu.VMEM((3, depth, width), jnp.float32),
            pltpu.VMEM((3, depth, width), jnp.float32),
            pltpu.VMEM((part, width), jnp.bfloat16),
            pltpu.VMEM((count, width), jnp.float32),
            pltpu.VMEM((width, count), jnp.bfloat16),
            pltpu.SemaphoreType.DMA((steps, 4)),
            pltpu.SemaphoreType.DMA((steps, 3)),
            pltpu.SemaphoreType.DMA,
        ],
        compiler_params=params(24),
        cost_estimate=pl.CostEstimate(
            flops=4 * count * depth * width, bytes_accessed=2 * count * depth + 24 * depth * width, transcendentals=0
        ),
        name="inner",
    )(*map(in_hbm, (tokens, weight, first, second, cots[0])), low_weight, *cots[1:])
    return got[:3], got[3], got[4:]


def times_transposed(left, right):
    return lax.dot_general(left, right, (((1,), (1,)), ((), ())), preferred_element_type=jnp.float32)


def arrived_kernel(rows, cols, tile, *refs):
    per_row = cols // rows
    block_refs, message_refs = refs[:per_row], refs[per_row:per_row + rows - 1]
    refs = refs[:per_row] + refs[per_row + rows - 1:]
    sum_refs = refs[per_row:per_row + rows - 1]
    own_ref = refs[per_row + rows - 1]
    weight_refs = refs[per_row + rows:per_row + rows + cols - 1]
    slot_ref, global_hbm, moment_hbm, sum_ref, last_ref, held_ref, prior_ref, keys_values_hbm = refs[-14:-6]
    blocks_ref, keys_values_ref, global_ref, moment_ref, sem, slot_sems = refs[-6:]
    row, col = lax.axis_index("row"), lax.axis_index("col")
    loads = [
        pltpu.make_async_copy(global_hbm, global_ref, slot_sems.at[0]),
        pltpu.make_async_copy(moment_hbm, moment_ref, slot_sems.at[1]),
    ]
    for load in loads:
        load.start()
    size, part = block_refs[0].shape[0], own_ref.shape[0]
    total = own_ref[...]
    for other_ref in sum_refs:
        total += other_ref[...].astype(jnp.float32)
    keys_values_ref[...] = total.astype(jnp.bfloat16)
    store = pltpu.make_async_copy(keys_values_ref, keys_values_hbm, sem)
    store.start()
    for k in range(per_row):
        column = mod(lax.rem(col, per_row) - k, per_row)
        blocks_ref[row * per_row + column] = block_refs[k][...]
        for j in range(1, rows):
            blocks_ref[mod(row - j, rows) * per_row + column] = message_refs[j - 1][pl.ds(k * size, size), :]
    last_ref[...] = blocks_ref[owner_of(col, cols - 1, cols)]
    left = [blocks_ref[owner_of(col, k, cols)] for k in range(cols - 1)]
    for start in range(0, weight_refs[0].shape[0], tile):
        features = pl.ds(start, tile)
        piece = None
        for k in range(0, cols - 1, 2):
            few = range(k, min(k + 2, cols - 1))
            product = times_transposed(
                jnp.concatenate([left[i] for i in few], axis=1),
                jnp.concatenate([weight_refs[i][features, :] for i in few], axis=1),
            )
            piece = product if piece is None else piece + product
        sum_ref[:, features] = piece
    slot, count = slot_ref[0], held_ref.shape[0]
    slots = global_ref.shape[0] // count
    for load, source_ref, out_ref in zip(loads, (global_ref, moment_ref), (held_ref, prior_ref)):
        load.wait()
        picked = source_ref[pl.ds(0, count, stride=slots), :]
        for i in range(1, slots):
            picked = jnp.where(slot == i, source_ref[pl.ds(i, count, stride=slots), :], picked)
        out_ref[...] = picked
    store.wait()


def arrived(blocks, messages, sums, own, weights, cols, global_params, outer_moment, group_slot):
    rows, per_row = len(messages) + 1, len(blocks)
    size, width = blocks[0].shape
    depth = weights[0].shape[0]
    held = jax.ShapeDtypeStruct((global_params.shape[1] // LANES, LANES), jnp.float32)
    return pl.pallas_call(
        functools.partial(arrived_kernel, rows, cols, min(512, depth)),
        out_shape=[
            jax.ShapeDtypeStruct((size, depth), jnp.float32),
            jax.ShapeDtypeStruct((size, width), jnp.bfloat16),
            held,
            held,
            jax.ShapeDtypeStruct(own.shape, jnp.bfloat16),
        ],
        in_specs=[WHOLE] * (per_row + 2 * rows - 1 + cols - 1) + [pl.BlockSpec(memory_space=pltpu.SMEM), HBM, HBM],
        out_specs=[WHOLE] * 4 + [HBM],
        scratch_shapes=[
            pltpu.VMEM((cols, size, width), jnp.bfloat16),
            pltpu.VMEM(own.shape, jnp.bfloat16),
            pltpu.VMEM((global_params.size // LANES, LANES), jnp.float32),
            pltpu.VMEM((global_params.size // LANES, LANES), jnp.float32),
            pltpu.SemaphoreType.DMA,
            pltpu.SemaphoreType.DMA((2,)),
        ],
        compiler_params=params(24),
        cost_estimate=pl.CostEstimate(
            flops=2 * size * depth * width * (cols - 1), bytes_accessed=4 * size * depth, transcendentals=0
        ),
        name="arrived",
    )(
        *blocks, *messages, *sums, own, *weights, group_slot, in_hbm(interleaved(global_params)), in_hbm(interleaved(outer_moment))
    )


def finish_kernel(tile, sum_ref, block_ref, weight_ref, out_hbm, out_ref, sems):
    stores = []
    for i, start in enumerate(range(0, weight_ref.shape[0], tile)):
        features = pl.ds(start, tile)
        piece = times_transposed(block_ref[...], weight_ref[features, :])
        out_ref[:, features] = (sum_ref[:, features] + piece).astype(jnp.bfloat16)
        stores.append(pltpu.make_async_copy(out_ref.at[:, features], out_hbm.at[:, features], sems.at[i]))
        stores[-1].start()
    for store in stores:
        store.wait()


def finish(total, block, weight):
    size, depth = total.shape
    tile = min(512, depth)
    return pl.pallas_call(
        functools.partial(finish_kernel, tile),
        out_shape=jax.ShapeDtypeStruct((size, depth), jnp.bfloat16),
        in_specs=[WHOLE] * 3,
        out_specs=HBM,
        scratch_shapes=[pltpu.VMEM((size, depth), jnp.bfloat16), pltpu.SemaphoreType.DMA((depth // tile,))],
        compiler_params=params(16),
        cost_estimate=pl.CostEstimate(
            flops=2 * size * depth * block.shape[1], bytes_accessed=6 * size * depth, transcendentals=0
        ),
        name="finish",
    )(total, block, weight)


def merge_kernel(replicas, sum_ref, other_ref, held_ref, prior_ref, new_global_hbm, new_outer_hbm, *scratch):
    new_global_ref, new_outer_ref, sems = scratch
    average = (sum_ref[...].astype(jnp.float32) + other_ref[...].astype(jnp.float32)) / replicas
    new_outer = NESTEROV * prior_ref[...] + average
    new_outer_ref[...] = new_outer
    outer_store = pltpu.make_async_copy(new_outer_ref, new_outer_hbm, sems.at[0])
    outer_store.start()
    new_global_ref[...] = held_ref[...] - OUTER_RATE * (average + NESTEROV * new_outer)
    global_store = pltpu.make_async_copy(new_global_ref, new_global_hbm, sems.at[1])
    global_store.start()
    outer_store.wait()
    global_store.wait()


def interleaved(x):
    slots, size = x.shape
    return x.reshape(slots, size // LANES, LANES).transpose(1, 0, 2).reshape(slots * size // LANES, LANES)


def outer_sums(low, axis, early):
    n = lax.axis_size(axis)
    if not is_power_of_two(n):
        return lax.psum(low, axis), jnp.zeros_like(low)
    bit = 1
    while True:
        other = lax.ppermute(low, axis, swap_pairs(n, bit))
        bit *= 2
        if bit >= n:
            return low, other
        other, _ = after(other, early)
        low = (low.astype(jnp.float32) + other.astype(jnp.float32)).astype(jnp.bfloat16)


def merge(low, other, held, prior, replicas):
    shape = jax.ShapeDtypeStruct(low.shape, jnp.float32)
    new_global, new_outer = pl.pallas_call(
        functools.partial(merge_kernel, replicas),
        out_shape=[shape, shape],
        in_specs=[WHOLE] * 4,
        out_specs=[HBM] * 2,
        scratch_shapes=[pltpu.VMEM(low.shape, jnp.float32)] * 2 + [pltpu.SemaphoreType.DMA((2,))],
        compiler_params=params(16),
        cost_estimate=pl.CostEstimate(flops=8 * low.size, bytes_accessed=8 * low.size, transcendentals=0),
        name="merge",
    )(low, other, held, prior)
    return new_global.reshape(-1), new_outer.reshape(-1)


def on_device(
    tokens,
    cotangent,
    weight,
    first_moment,
    second_moment,
    outer_delta,
    global_params,
    outer_moment,
    group_slot,
):
    rows, cols = lax.axis_size("row"), lax.axis_size("col")
    replicas = lax.axis_size("rep")
    per_row = cols // rows
    cots = shifted(cotangent, "row")
    low_weight = rounded(weight[0])
    low, chunks = prepare(cotangent, outer_delta.reshape(-1, LANES), per_row)
    received = [lax.ppermute(chunks[k], ("row", "col"), chunk_pairs(rows, cols, per_row, k)) for k in range(per_row)]
    (new_weight, new_first, new_second), own, sends = inner(
        tokens, weight[0], first_moment[0], second_moment[0], cots, low_weight
    )
    weights = gather_offsets(low_weight, "col", sends)
    low, other = outer_sums(low, "rep", (sends, weights[1], weights[cols // 2]))
    received, _ = after(received, weights[cols // 2])
    sums = [lax.ppermute(m, "row", shift_pairs(rows, k + 1)) for k, m in enumerate(sends)]
    messages = [lax.ppermute(pack(received), "row", shift_pairs(rows, k)) for k in range(1, rows)]
    total, block, held, prior, keys_values = arrived(
        received, messages, sums, own, weights[:-1], cols, global_params, outer_moment, group_slot
    )
    new_global, new_outer = merge(low, other, held, prior, replicas)
    last, _ = after(weights[-1], (new_outer, total))
    input_grad = finish(total, block, last)
    return (keys_values, input_grad, new_weight[None], new_first[None], new_second[None], new_global, new_outer)


def solution(mesh):
    in_specs = (
        P("rep", "row"),
        P(("rep", "row"), "col"),
        P("rep", "row", "col"),
        P("rep", "row", "col"),
        P("rep", "row", "col"),
        P("rep", ("row", "col")),
        P(None, ("row", "col")),
        P(None, ("row", "col")),
        P(),
    )
    out_specs = (
        P(("rep", "row"), "col"),
        P(("rep", "col"), "row"),
        P("rep", "row", "col"),
        P("rep", "row", "col"),
        P("rep", "row", "col"),
        P(("row", "col")),
        P(("row", "col")),
    )
    return jax.shard_map(
        on_device, mesh=mesh, in_specs=in_specs, out_specs=out_specs, check_vma=False
    )
```

```python
import functools

import jax
import jax.numpy as jnp
from jax import lax
from jax.experimental import pallas as pl
from jax.experimental.pallas import tpu as pltpu
from jax.sharding import PartitionSpec as P

BETA_ONE = 0.9
BETA_TWO = 0.95
INNER_RATE = 0.0003
WEIGHT_DECAY = 0.1
EPSILON = 1e-08
OUTER_RATE = 0.7
NESTEROV = 0.9
LANES = 128

WHOLE = pl.BlockSpec(memory_space=pltpu.VMEM)
HBM = pl.BlockSpec(memory_space=pltpu.HBM)


def params(mebibytes):
    return pltpu.CompilerParams(vmem_limit_bytes=mebibytes * 1024 * 1024)


def after(x, others):
    return lax.optimization_barrier((x, others))


def in_hbm(x):
    return pltpu.with_memory_space_constraint(x, pltpu.HBM)


def is_power_of_two(n):
    return n & (n - 1) == 0


def swap_pairs(n, bit):
    return [(i, i ^ bit) for i in range(n)]


def shift_pairs(n, k):
    return [(i, (i + k) % n) for i in range(n)]


def mod(value, n):
    return lax.rem(value + n, n)


FIRST_CYCLE = [(0, 2), (2, 3), (3, 1), (1, 0)]
SECOND_CYCLE = [(0, 1), (1, 3), (3, 2), (2, 0)]
TO_ENDS = [(1, 0), (2, 3)]
INNER = [(1, 2), (2, 1)]


def gather_blocks(block, axis, early):
    n = lax.axis_size(axis)
    if n == len(FIRST_CYCLE):
        near = lax.ppermute(block, axis, FIRST_CYCLE)
        far = lax.ppermute(block, axis, SECOND_CYCLE)
        passed, _ = after(near, early)
        ends = lax.ppermute(passed, axis, TO_ENDS)
        own, _ = after(block, passed)
        return [block, near, far], [ends, lax.ppermute(own, axis, INNER)]
    have = [block]
    for k in range(1, n):
        have.append(lax.ppermute(have[k - 1], axis, shift_pairs(n, n - 1)))
    return have[:-1], have[-1:]


def owner_of(me, k, n):
    if n == len(FIRST_CYCLE):
        return lax.rem((k + 1) * (me + 1), n + 1) - 1
    return mod(me + k, n)


def shifted(block, axis):
    n = lax.axis_size(axis)
    return [block] + [lax.ppermute(block, axis, shift_pairs(n, k)) for k in range(1, n)]


def chunk_pairs(rows, cols, per_row, k):
    pairs = []
    for r in range(rows):
        for c in range(cols):
            pairs.append((r * cols + c, (c // per_row) * cols + r * per_row + (c + k) % per_row))
    return pairs


def round_kernel(pieces, source_hbm, out_ref, source_ref, sems):
    size = source_ref.shape[0] // pieces
    parts = [pl.ds(i * size, size) for i in range(pieces)]
    loads = [pltpu.make_async_copy(source_hbm.at[p, :], source_ref.at[p, :], sems.at[i]) for i, p in enumerate(parts)]
    for load in loads:
        load.start()
    for load, part in zip(loads, parts):
        load.wait()
        out_ref[part, :] = source_ref[part, :].astype(jnp.bfloat16)


def rounded(x):
    pieces = 2
    return pl.pallas_call(
        functools.partial(round_kernel, pieces),
        out_shape=jax.ShapeDtypeStruct(x.shape, jnp.bfloat16),
        in_specs=[HBM],
        out_specs=WHOLE,
        scratch_shapes=[pltpu.VMEM(x.shape, jnp.float32), pltpu.SemaphoreType.DMA((pieces,))],
        compiler_params=params(16),
        cost_estimate=pl.CostEstimate(flops=0, bytes_accessed=6 * x.size, transcendentals=0),
        name="rounded",
    )(in_hbm(x))


def prepare_kernel(per_row, cot_hbm, delta_hbm, low_delta_ref, *refs):
    chunk_refs = refs[:per_row]
    delta_ref, sem, chunk_sems = refs[per_row:]
    size = chunk_refs[0].shape[0]
    col = lax.axis_index("col")
    load = pltpu.make_async_copy(delta_hbm, delta_ref, sem)
    load.start()
    chunks = []
    for k in range(per_row):
        start = pl.multiple_of(lax.rem(col + k, per_row) * size, size)
        chunks.append(pltpu.make_async_copy(cot_hbm.at[pl.ds(start, size), :], chunk_refs[k], chunk_sems.at[k]))
        chunks[-1].start()
    load.wait()
    low_delta_ref[...] = delta_ref[...].astype(jnp.bfloat16)
    for copy in chunks:
        copy.wait()


def prepare(cotangent, delta, per_row):
    chunk = cotangent.shape[0] // per_row
    shape = lambda *s: jax.ShapeDtypeStruct(s, jnp.bfloat16)
    outs = [shape(*delta.shape)] + [shape(chunk, cotangent.shape[1])] * per_row
    got = pl.pallas_call(
        functools.partial(prepare_kernel, per_row),
        out_shape=outs,
        in_specs=[HBM] * 2,
        out_specs=[WHOLE] * len(outs),
        scratch_shapes=[
            pltpu.VMEM(delta.shape, jnp.float32),
            pltpu.SemaphoreType.DMA,
            pltpu.SemaphoreType.DMA((per_row,)),
        ],
        compiler_params=params(16),
        cost_estimate=pl.CostEstimate(flops=0, bytes_accessed=6 * delta.size, transcendentals=0),
        name="prepare",
    )(*map(in_hbm, (cotangent, delta)))
    return got[0], got[1:]


def pack_kernel(*refs):
    size = refs[0].shape[0]
    for k, block_ref in enumerate(refs[:-1]):
        refs[-1][pl.ds(k * size, size), :] = block_ref[...]


def pack(blocks):
    size, width = blocks[0].shape
    return pl.pallas_call(
        pack_kernel,
        out_shape=jax.ShapeDtypeStruct((len(blocks) * size, width), jnp.bfloat16),
        in_specs=[WHOLE] * len(blocks),
        out_specs=WHOLE,
        compiler_params=params(16),
        cost_estimate=pl.CostEstimate(flops=0, bytes_accessed=4 * len(blocks) * size * width, transcendentals=0),
        name="pack",
    )(*blocks)


def inner_kernel(rows, steps, *refs):
    tokens_hbm, weight_hbm, first_hbm, second_hbm, cot_hbm, low_weight_ref = refs[:6]
    cot_refs = refs[6:5 + rows]
    new_weight_hbm, new_first_hbm, new_second_hbm, own_ref = refs[5 + rows:9 + rows]
    send_refs = refs[9 + rows:8 + 2 * rows]
    tokens_ref, state_ref, fresh_ref, cot_ref, total_ref, turned_ref, sems, out_sems, cot_sem = refs[-9:]
    row = lax.axis_index("row")
    part = cot_ref.shape[0]
    tile = tokens_ref.shape[1] // steps
    block = [pl.ds(s * tile, tile) for s in range(steps)]
    states = (weight_hbm, first_hbm, second_hbm)
    fresh = (new_weight_hbm, new_first_hbm, new_second_hbm)

    cot_load = pltpu.make_async_copy(cot_hbm, cot_ref, cot_sem)
    token_loads, state_loads, stores = [], [], []
    for s in range(steps):
        token_loads.append(pltpu.make_async_copy(tokens_hbm.at[:, block[s]], tokens_ref.at[:, block[s]], sems.at[s, 3]))
        state_loads.append([
            pltpu.make_async_copy(state.at[block[s], :], state_ref.at[i, block[s], :], sems.at[s, i])
            for i, state in enumerate(states)
        ])
        stores.append([
            pltpu.make_async_copy(fresh_ref.at[i, block[s], :], out.at[block[s], :], out_sems.at[s, i])
            for i, out in enumerate(fresh)
        ])
    cot_load.start()
    for s in range(steps):
        token_loads[s].start()
        for load in state_loads[s]:
            load.start()

    for k in range(1, rows):
        start = pl.multiple_of(mod(row - k, rows) * part, part)
        turned_ref[:, pl.ds(start, part)] = cot_refs[k - 1][...].T
    cot_load.wait()
    turned_ref[:, pl.ds(pl.multiple_of(row * part, part), part)] = cot_ref[...].T

    for s in range(steps):
        token_loads[s].wait()
        tokens = tokens_ref[:, block[s]]
        product = jnp.dot(tokens, low_weight_ref[block[s], :], preferred_element_type=jnp.float32)
        if s == 0:
            total_ref[...] = product
        else:
            total_ref[...] += product
        gradient = jnp.dot(turned_ref[...], tokens, preferred_element_type=jnp.float32).T
        for load in state_loads[s]:
            load.wait()
        weight = state_ref[0, block[s], :]
        first = BETA_ONE * state_ref[1, block[s], :] + (1.0 - BETA_ONE) * gradient
        second = BETA_TWO * state_ref[2, block[s], :] + (1.0 - BETA_TWO) * gradient * gradient
        fresh_ref[0, block[s], :] = weight - INNER_RATE * (
            first / (jnp.sqrt(second) + EPSILON) + WEIGHT_DECAY * weight
        )
        fresh_ref[1, block[s], :] = first
        fresh_ref[2, block[s], :] = second
        for store in stores[s]:
            store.start()

    own_ref[...] = total_ref[pl.ds(pl.multiple_of(row * part, part), part), :]
    for k in range(1, rows):
        start = pl.multiple_of(mod(row + k - rows, rows) * part, part)
        send_refs[k - 1][...] = total_ref[pl.ds(start, part), :].astype(jnp.bfloat16)
    for s in range(steps):
        for store in stores[s]:
            store.wait()


def inner(tokens, weight, first, second, cots, low_weight):
    rows = len(cots)
    count, depth = tokens.shape
    width = weight.shape[1]
    part = count // rows
    steps = depth // min(512, depth)
    full = jax.ShapeDtypeStruct((depth, width), jnp.float32)
    outs = [
        full,
        full,
        full,
        jax.ShapeDtypeStruct((part, width), jnp.float32),
    ] + [jax.ShapeDtypeStruct((part, width), jnp.bfloat16)] * (rows - 1)
    got = pl.pallas_call(
        functools.partial(inner_kernel, rows, steps),
        in_specs=[HBM] * 5 + [WHOLE] * rows,
        out_specs=[HBM] * 3 + [WHOLE] * rows,
        out_shape=outs,
        scratch_shapes=[
            pltpu.VMEM((count, depth), jnp.bfloat16),
            pltpu.VMEM((3, depth, width), jnp.float32),
            pltpu.VMEM((3, depth, width), jnp.float32),
            pltpu.VMEM((part, width), jnp.bfloat16),
            pltpu.VMEM((count, width), jnp.float32),
            pltpu.VMEM((width, count), jnp.bfloat16),
            pltpu.SemaphoreType.DMA((steps, 4)),
            pltpu.SemaphoreType.DMA((steps, 3)),
            pltpu.SemaphoreType.DMA,
        ],
        compiler_params=params(24),
        cost_estimate=pl.CostEstimate(
            flops=4 * count * depth * width, bytes_accessed=2 * count * depth + 24 * depth * width, transcendentals=0
        ),
        name="inner",
    )(*map(in_hbm, (tokens, weight, first, second, cots[0])), low_weight, *cots[1:])
    return got[:3], got[3], got[4:]


def times_transposed(left, right):
    return lax.dot_general(left, right, (((1,), (1,)), ((), ())), preferred_element_type=jnp.float32)


def arrived_kernel(rows, cols, tile, *refs):
    per_row = cols // rows
    block_refs, message_refs = refs[:per_row], refs[per_row:per_row + rows - 1]
    refs = refs[:per_row] + refs[per_row + rows - 1:]
    sum_refs = refs[per_row:per_row + rows - 1]
    own_ref = refs[per_row + rows - 1]
    weight_refs = refs[per_row + rows:per_row + rows + cols - 1]
    slot_ref, global_hbm, moment_hbm, sum_ref, last_ref, held_ref, prior_ref, keys_values_hbm = refs[-14:-6]
    blocks_ref, keys_values_ref, global_ref, moment_ref, sem, slot_sems = refs[-6:]
    row, col = lax.axis_index("row"), lax.axis_index("col")
    loads = [
        pltpu.make_async_copy(global_hbm, global_ref, slot_sems.at[0]),
        pltpu.make_async_copy(moment_hbm, moment_ref, slot_sems.at[1]),
    ]
    for load in loads:
        load.start()
    size, part = block_refs[0].shape[0], own_ref.shape[0]
    total = own_ref[...]
    for other_ref in sum_refs:
        total += other_ref[...].astype(jnp.float32)
    keys_values_ref[...] = total.astype(jnp.bfloat16)
    store = pltpu.make_async_copy(keys_values_ref, keys_values_hbm, sem)
    store.start()
    for k in range(per_row):
        column = mod(lax.rem(col, per_row) - k, per_row)
        blocks_ref[row * per_row + column] = block_refs[k][...]
        for j in range(1, rows):
            blocks_ref[mod(row - j, rows) * per_row + column] = message_refs[j - 1][pl.ds(k * size, size), :]
    last_ref[...] = blocks_ref[owner_of(col, cols - 1, cols)]
    left = [blocks_ref[owner_of(col, k, cols)] for k in range(cols - 1)]
    for start in range(0, weight_refs[0].shape[0], tile):
        features = pl.ds(start, tile)
        piece = None
        for k in range(0, cols - 1, 2):
            few = range(k, min(k + 2, cols - 1))
            product = times_transposed(
                jnp.concatenate([left[i] for i in few], axis=1),
                jnp.concatenate([weight_refs[i][features, :] for i in few], axis=1),
            )
            piece = product if piece is None else piece + product
        sum_ref[:, features] = piece
    slot, count = slot_ref[0], held_ref.shape[0]
    slots = global_ref.shape[0] // count
    for load, source_ref, out_ref in zip(loads, (global_ref, moment_ref), (held_ref, prior_ref)):
        load.wait()
        picked = source_ref[pl.ds(0, count, stride=slots), :]
        for i in range(1, slots):
            picked = jnp.where(slot == i, source_ref[pl.ds(i, count, stride=slots), :], picked)
        out_ref[...] = picked
    store.wait()


def arrived(blocks, messages, sums, own, weights, cols, global_params, outer_moment, group_slot):
    rows, per_row = len(messages) + 1, len(blocks)
    size, width = blocks[0].shape
    depth = weights[0].shape[0]
    held = jax.ShapeDtypeStruct((global_params.shape[1] // LANES, LANES), jnp.float32)
    return pl.pallas_call(
        functools.partial(arrived_kernel, rows, cols, min(512, depth)),
        out_shape=[
            jax.ShapeDtypeStruct((size, depth), jnp.float32),
            jax.ShapeDtypeStruct((size, width), jnp.bfloat16),
            held,
            held,
            jax.ShapeDtypeStruct(own.shape, jnp.bfloat16),
        ],
        in_specs=[WHOLE] * (per_row + 2 * rows - 1 + cols - 1) + [pl.BlockSpec(memory_space=pltpu.SMEM), HBM, HBM],
        out_specs=[WHOLE] * 4 + [HBM],
        scratch_shapes=[
            pltpu.VMEM((cols, size, width), jnp.bfloat16),
            pltpu.VMEM(own.shape, jnp.bfloat16),
            pltpu.VMEM((global_params.size // LANES, LANES), jnp.float32),
            pltpu.VMEM((global_params.size // LANES, LANES), jnp.float32),
            pltpu.SemaphoreType.DMA,
            pltpu.SemaphoreType.DMA((2,)),
        ],
        compiler_params=params(24),
        cost_estimate=pl.CostEstimate(
            flops=2 * size * depth * width * (cols - 1), bytes_accessed=4 * size * depth, transcendentals=0
        ),
        name="arrived",
    )(
        *blocks, *messages, *sums, own, *weights, group_slot, in_hbm(interleaved(global_params)), in_hbm(interleaved(outer_moment))
    )


def finish_kernel(tile, count, sum_ref, block_ref, *refs):
    weight_refs = refs[:count]
    out_hbm, out_ref, sems = refs[count:]
    col = lax.axis_index("col")
    outside = (col == 0) | (col == lax.axis_size("col") - 1)
    stores = []
    for i, start in enumerate(range(0, sum_ref.shape[1], tile)):
        features = pl.ds(start, tile)
        weight = weight_refs[0][features, :]
        if count > 1:
            weight = jnp.where(outside, weight, weight_refs[1][features, :])
        piece = times_transposed(block_ref[...], weight)
        out_ref[:, features] = (sum_ref[:, features] + piece).astype(jnp.bfloat16)
        stores.append(pltpu.make_async_copy(out_ref.at[:, features], out_hbm.at[:, features], sems.at[i]))
        stores[-1].start()
    for store in stores:
        store.wait()


def finish(total, block, weights):
    size, depth = total.shape
    tile = min(512, depth)
    return pl.pallas_call(
        functools.partial(finish_kernel, tile, len(weights)),
        out_shape=jax.ShapeDtypeStruct((size, depth), jnp.bfloat16),
        in_specs=[WHOLE] * (2 + len(weights)),
        out_specs=HBM,
        scratch_shapes=[pltpu.VMEM((size, depth), jnp.bfloat16), pltpu.SemaphoreType.DMA((depth // tile,))],
        compiler_params=params(16),
        cost_estimate=pl.CostEstimate(
            flops=2 * size * depth * block.shape[1], bytes_accessed=6 * size * depth, transcendentals=0
        ),
        name="finish",
    )(total, block, *weights)


def merge_kernel(replicas, sum_ref, other_ref, held_ref, prior_ref, new_global_hbm, new_outer_hbm, *scratch):
    new_global_ref, new_outer_ref, sems = scratch
    average = (sum_ref[...].astype(jnp.float32) + other_ref[...].astype(jnp.float32)) / replicas
    new_outer = NESTEROV * prior_ref[...] + average
    new_outer_ref[...] = new_outer
    outer_store = pltpu.make_async_copy(new_outer_ref, new_outer_hbm, sems.at[0])
    outer_store.start()
    new_global_ref[...] = held_ref[...] - OUTER_RATE * (average + NESTEROV * new_outer)
    global_store = pltpu.make_async_copy(new_global_ref, new_global_hbm, sems.at[1])
    global_store.start()
    outer_store.wait()
    global_store.wait()


def interleaved(x):
    slots, size = x.shape
    return x.reshape(slots, size // LANES, LANES).transpose(1, 0, 2).reshape(slots * size // LANES, LANES)


def outer_sums(low, axis, early):
    n = lax.axis_size(axis)
    if not is_power_of_two(n):
        return lax.psum(low, axis), jnp.zeros_like(low)
    bit = 1
    while True:
        other = lax.ppermute(low, axis, swap_pairs(n, bit))
        bit *= 2
        if bit >= n:
            return low, other
        other, _ = after(other, early)
        low = (low.astype(jnp.float32) + other.astype(jnp.float32)).astype(jnp.bfloat16)


def merge(low, other, held, prior, replicas):
    shape = jax.ShapeDtypeStruct(low.shape, jnp.float32)
    new_global, new_outer = pl.pallas_call(
        functools.partial(merge_kernel, replicas),
        out_shape=[shape, shape],
        in_specs=[WHOLE] * 4,
        out_specs=[HBM] * 2,
        scratch_shapes=[pltpu.VMEM(low.shape, jnp.float32)] * 2 + [pltpu.SemaphoreType.DMA((2,))],
        compiler_params=params(16),
        cost_estimate=pl.CostEstimate(flops=8 * low.size, bytes_accessed=8 * low.size, transcendentals=0),
        name="merge",
    )(low, other, held, prior)
    return new_global.reshape(-1), new_outer.reshape(-1)


def on_device(
    tokens,
    cotangent,
    weight,
    first_moment,
    second_moment,
    outer_delta,
    global_params,
    outer_moment,
    group_slot,
):
    rows, cols = lax.axis_size("row"), lax.axis_size("col")
    replicas = lax.axis_size("rep")
    per_row = cols // rows
    cots = shifted(cotangent, "row")
    low_weight = rounded(weight[0])
    low, chunks = prepare(cotangent, outer_delta.reshape(-1, LANES), per_row)
    received = [lax.ppermute(chunks[k], ("row", "col"), chunk_pairs(rows, cols, per_row, k)) for k in range(per_row)]
    (new_weight, new_first, new_second), own, sends = inner(
        tokens, weight[0], first_moment[0], second_moment[0], cots, low_weight
    )
    weights, last = gather_blocks(low_weight, "col", sends)
    low, other = outer_sums(low, "rep", (sends, weights[1:]))
    received, _ = after(received, weights[1])
    sums = [lax.ppermute(m, "row", shift_pairs(rows, k + 1)) for k, m in enumerate(sends)]
    messages = [lax.ppermute(pack(received), "row", shift_pairs(rows, k)) for k in range(1, rows)]
    total, block, held, prior, keys_values = arrived(
        received, messages, sums, own, weights, cols, global_params, outer_moment, group_slot
    )
    new_global, new_outer = merge(low, other, held, prior, replicas)
    last, _ = after(last, (new_outer, total))
    input_grad = finish(total, block, last)
    return (keys_values, input_grad, new_weight[None], new_first[None], new_second[None], new_global, new_outer)


def solution(mesh):
    in_specs = (
        P("rep", "row"),
        P(("rep", "row"), "col"),
        P("rep", "row", "col"),
        P("rep", "row", "col"),
        P("rep", "row", "col"),
        P("rep", ("row", "col")),
        P(None, ("row", "col")),
        P(None, ("row", "col")),
        P(),
    )
    out_specs = (
        P(("rep", "row"), "col"),
        P(("rep", "col"), "row"),
        P("rep", "row", "col"),
        P("rep", "row", "col"),
        P("rep", "row", "col"),
        P(("row", "col")),
        P(("row", "col")),
    )
    return jax.shard_map(
        on_device, mesh=mesh, in_specs=in_specs, out_specs=out_specs, check_vma=False
    )
```

```python
import functools

import jax
import jax.numpy as jnp
from jax import lax
from jax.experimental import pallas as pl
from jax.experimental.pallas import tpu as pltpu
from jax.sharding import PartitionSpec as P

BETA_ONE = 0.9
BETA_TWO = 0.95
INNER_RATE = 0.0003
WEIGHT_DECAY = 0.1
EPSILON = 1e-08
OUTER_RATE = 0.7
NESTEROV = 0.9
LANES = 128

WHOLE = pl.BlockSpec(memory_space=pltpu.VMEM)
HBM = pl.BlockSpec(memory_space=pltpu.HBM)


def params(mebibytes):
    return pltpu.CompilerParams(vmem_limit_bytes=mebibytes * 1024 * 1024)


def after(x, others):
    return lax.optimization_barrier((x, others))


def in_hbm(x):
    return pltpu.with_memory_space_constraint(x, pltpu.HBM)


def is_power_of_two(n):
    return n & (n - 1) == 0


def swap_pairs(n, bit):
    return [(i, i ^ bit) for i in range(n)]


def shift_pairs(n, k):
    return [(i, (i + k) % n) for i in range(n)]


def mod(value, n):
    return lax.rem(value + n, n)


FIRST_CYCLE = [(0, 2), (2, 3), (3, 1), (1, 0)]
SECOND_CYCLE = [(0, 1), (1, 3), (3, 2), (2, 0)]
TO_ENDS = [(1, 0), (2, 3)]
INNER = [(1, 2), (2, 1)]


def gather_blocks(block, axis, early):
    n = lax.axis_size(axis)
    if n == len(FIRST_CYCLE):
        near = lax.ppermute(block, axis, FIRST_CYCLE)
        far = lax.ppermute(block, axis, SECOND_CYCLE)
        passed, _ = after(near, early)
        ends = lax.ppermute(passed, axis, TO_ENDS)
        own, _ = after(block, (passed, far))
        return [block, near, far], [ends, lax.ppermute(own, axis, INNER)]
    have = [block]
    for k in range(1, n):
        have.append(lax.ppermute(have[k - 1], axis, shift_pairs(n, n - 1)))
    return have[:-1], have[-1:]


def owner_of(me, k, n):
    if n == len(FIRST_CYCLE):
        return lax.rem((k + 1) * (me + 1), n + 1) - 1
    return mod(me + k, n)


def shifted(block, axis):
    n = lax.axis_size(axis)
    return [block] + [lax.ppermute(block, axis, shift_pairs(n, k)) for k in range(1, n)]


def chunk_pairs(rows, cols, per_row, k):
    pairs = []
    for r in range(rows):
        for c in range(cols):
            pairs.append((r * cols + c, (c // per_row) * cols + r * per_row + (c + k) % per_row))
    return pairs


def round_kernel(pieces, source_hbm, out_ref, source_ref, sems):
    size = source_ref.shape[0] // pieces
    parts = [pl.ds(i * size, size) for i in range(pieces)]
    loads = [pltpu.make_async_copy(source_hbm.at[p, :], source_ref.at[p, :], sems.at[i]) for i, p in enumerate(parts)]
    for load in loads:
        load.start()
    for load, part in zip(loads, parts):
        load.wait()
        out_ref[part, :] = source_ref[part, :].astype(jnp.bfloat16)


def rounded(x):
    pieces = 2
    return pl.pallas_call(
        functools.partial(round_kernel, pieces),
        out_shape=jax.ShapeDtypeStruct(x.shape, jnp.bfloat16),
        in_specs=[HBM],
        out_specs=WHOLE,
        scratch_shapes=[pltpu.VMEM(x.shape, jnp.float32), pltpu.SemaphoreType.DMA((pieces,))],
        compiler_params=params(16),
        cost_estimate=pl.CostEstimate(flops=0, bytes_accessed=6 * x.size, transcendentals=0),
        name="rounded",
    )(in_hbm(x))


def prepare_kernel(per_row, cot_hbm, delta_hbm, low_delta_ref, *refs):
    chunk_refs = refs[:per_row]
    delta_ref, sem, chunk_sems = refs[per_row:]
    size = chunk_refs[0].shape[0]
    col = lax.axis_index("col")
    load = pltpu.make_async_copy(delta_hbm, delta_ref, sem)
    load.start()
    chunks = []
    for k in range(per_row):
        start = pl.multiple_of(lax.rem(col + k, per_row) * size, size)
        chunks.append(pltpu.make_async_copy(cot_hbm.at[pl.ds(start, size), :], chunk_refs[k], chunk_sems.at[k]))
        chunks[-1].start()
    load.wait()
    low_delta_ref[...] = delta_ref[...].astype(jnp.bfloat16)
    for copy in chunks:
        copy.wait()


def prepare(cotangent, delta, per_row):
    chunk = cotangent.shape[0] // per_row
    shape = lambda *s: jax.ShapeDtypeStruct(s, jnp.bfloat16)
    outs = [shape(*delta.shape)] + [shape(chunk, cotangent.shape[1])] * per_row
    got = pl.pallas_call(
        functools.partial(prepare_kernel, per_row),
        out_shape=outs,
        in_specs=[HBM] * 2,
        out_specs=[WHOLE] * len(outs),
        scratch_shapes=[
            pltpu.VMEM(delta.shape, jnp.float32),
            pltpu.SemaphoreType.DMA,
            pltpu.SemaphoreType.DMA((per_row,)),
        ],
        compiler_params=params(16),
        cost_estimate=pl.CostEstimate(flops=0, bytes_accessed=6 * delta.size, transcendentals=0),
        name="prepare",
    )(*map(in_hbm, (cotangent, delta)))
    return got[0], got[1:]


def pack_kernel(*refs):
    size = refs[0].shape[0]
    for k, block_ref in enumerate(refs[:-1]):
        refs[-1][pl.ds(k * size, size), :] = block_ref[...]


def pack(blocks):
    size, width = blocks[0].shape
    return pl.pallas_call(
        pack_kernel,
        out_shape=jax.ShapeDtypeStruct((len(blocks) * size, width), jnp.bfloat16),
        in_specs=[WHOLE] * len(blocks),
        out_specs=WHOLE,
        compiler_params=params(16),
        cost_estimate=pl.CostEstimate(flops=0, bytes_accessed=4 * len(blocks) * size * width, transcendentals=0),
        name="pack",
    )(*blocks)


def inner_kernel(rows, steps, *refs):
    tokens_hbm, weight_hbm, first_hbm, second_hbm, cot_hbm, low_weight_ref = refs[:6]
    cot_refs = refs[6:5 + rows]
    new_weight_hbm, new_first_hbm, new_second_hbm, own_ref = refs[5 + rows:9 + rows]
    send_refs = refs[9 + rows:8 + 2 * rows]
    tokens_ref, state_ref, fresh_ref, cot_ref, total_ref, turned_ref, sems, out_sems, cot_sem = refs[-9:]
    row = lax.axis_index("row")
    part = cot_ref.shape[0]
    tile = tokens_ref.shape[1] // steps
    block = [pl.ds(s * tile, tile) for s in range(steps)]
    states = (weight_hbm, first_hbm, second_hbm)
    fresh = (new_weight_hbm, new_first_hbm, new_second_hbm)

    cot_load = pltpu.make_async_copy(cot_hbm, cot_ref, cot_sem)
    token_loads, state_loads, stores = [], [], []
    for s in range(steps):
        token_loads.append(pltpu.make_async_copy(tokens_hbm.at[:, block[s]], tokens_ref.at[:, block[s]], sems.at[s, 3]))
        state_loads.append([
            pltpu.make_async_copy(state.at[block[s], :], state_ref.at[i, block[s], :], sems.at[s, i])
            for i, state in enumerate(states)
        ])
        stores.append([
            pltpu.make_async_copy(fresh_ref.at[i, block[s], :], out.at[block[s], :], out_sems.at[s, i])
            for i, out in enumerate(fresh)
        ])
    cot_load.start()
    for s in range(steps):
        token_loads[s].start()
        for load in state_loads[s]:
            load.start()

    for k in range(1, rows):
        start = pl.multiple_of(mod(row - k, rows) * part, part)
        turned_ref[:, pl.ds(start, part)] = cot_refs[k - 1][...].T
    cot_load.wait()
    turned_ref[:, pl.ds(pl.multiple_of(row * part, part), part)] = cot_ref[...].T

    for s in range(steps):
        token_loads[s].wait()
        tokens = tokens_ref[:, block[s]]
        product = jnp.dot(tokens, low_weight_ref[block[s], :], preferred_element_type=jnp.float32)
        if s == 0:
            total_ref[...] = product
        else:
            total_ref[...] += product
        gradient = jnp.dot(turned_ref[...], tokens, preferred_element_type=jnp.float32).T
        for load in state_loads[s]:
            load.wait()
        weight = state_ref[0, block[s], :]
        first = BETA_ONE * state_ref[1, block[s], :] + (1.0 - BETA_ONE) * gradient
        second = BETA_TWO * state_ref[2, block[s], :] + (1.0 - BETA_TWO) * gradient * gradient
        fresh_ref[0, block[s], :] = weight - INNER_RATE * (
            first / (jnp.sqrt(second) + EPSILON) + WEIGHT_DECAY * weight
        )
        fresh_ref[1, block[s], :] = first
        fresh_ref[2, block[s], :] = second
        for store in stores[s]:
            store.start()

    own_ref[...] = total_ref[pl.ds(pl.multiple_of(row * part, part), part), :]
    for k in range(1, rows):
        start = pl.multiple_of(mod(row + k - rows, rows) * part, part)
        send_refs[k - 1][...] = total_ref[pl.ds(start, part), :].astype(jnp.bfloat16)
    for s in range(steps):
        for store in stores[s]:
            store.wait()


def inner(tokens, weight, first, second, cots, low_weight):
    rows = len(cots)
    count, depth = tokens.shape
    width = weight.shape[1]
    part = count // rows
    steps = depth // min(512, depth)
    full = jax.ShapeDtypeStruct((depth, width), jnp.float32)
    outs = [
        full,
        full,
        full,
        jax.ShapeDtypeStruct((part, width), jnp.float32),
    ] + [jax.ShapeDtypeStruct((part, width), jnp.bfloat16)] * (rows - 1)
    got = pl.pallas_call(
        functools.partial(inner_kernel, rows, steps),
        in_specs=[HBM] * 5 + [WHOLE] * rows,
        out_specs=[HBM] * 3 + [WHOLE] * rows,
        out_shape=outs,
        scratch_shapes=[
            pltpu.VMEM((count, depth), jnp.bfloat16),
            pltpu.VMEM((3, depth, width), jnp.float32),
            pltpu.VMEM((3, depth, width), jnp.float32),
            pltpu.VMEM((part, width), jnp.bfloat16),
            pltpu.VMEM((count, width), jnp.float32),
            pltpu.VMEM((width, count), jnp.bfloat16),
            pltpu.SemaphoreType.DMA((steps, 4)),
            pltpu.SemaphoreType.DMA((steps, 3)),
            pltpu.SemaphoreType.DMA,
        ],
        compiler_params=params(24),
        cost_estimate=pl.CostEstimate(
            flops=4 * count * depth * width, bytes_accessed=2 * count * depth + 24 * depth * width, transcendentals=0
        ),
        name="inner",
    )(*map(in_hbm, (tokens, weight, first, second, cots[0])), low_weight, *cots[1:])
    return got[:3], got[3], got[4:]


def times_transposed(left, right):
    return lax.dot_general(left, right, (((1,), (1,)), ((), ())), preferred_element_type=jnp.float32)


def arrived_kernel(rows, cols, tile, *refs):
    per_row = cols // rows
    block_refs, message_refs = refs[:per_row], refs[per_row:per_row + rows - 1]
    refs = refs[:per_row] + refs[per_row + rows - 1:]
    sum_refs = refs[per_row:per_row + rows - 1]
    own_ref = refs[per_row + rows - 1]
    weight_refs = refs[per_row + rows:per_row + rows + cols - 1]
    slot_ref, global_hbm, moment_hbm, sum_ref, last_ref, held_ref, prior_ref, keys_values_hbm = refs[-14:-6]
    blocks_ref, keys_values_ref, global_ref, moment_ref, sem, slot_sems = refs[-6:]
    row, col = lax.axis_index("row"), lax.axis_index("col")
    loads = [
        pltpu.make_async_copy(global_hbm, global_ref, slot_sems.at[0]),
        pltpu.make_async_copy(moment_hbm, moment_ref, slot_sems.at[1]),
    ]
    for load in loads:
        load.start()
    size, part = block_refs[0].shape[0], own_ref.shape[0]
    total = own_ref[...]
    for other_ref in sum_refs:
        total += other_ref[...].astype(jnp.float32)
    keys_values_ref[...] = total.astype(jnp.bfloat16)
    store = pltpu.make_async_copy(keys_values_ref, keys_values_hbm, sem)
    store.start()
    for k in range(per_row):
        column = mod(lax.rem(col, per_row) - k, per_row)
        blocks_ref[row * per_row + column] = block_refs[k][...]
        for j in range(1, rows):
            blocks_ref[mod(row - j, rows) * per_row + column] = message_refs[j - 1][pl.ds(k * size, size), :]
    last_ref[...] = blocks_ref[owner_of(col, cols - 1, cols)]
    left = [blocks_ref[owner_of(col, k, cols)] for k in range(cols - 1)]
    for start in range(0, weight_refs[0].shape[0], tile):
        features = pl.ds(start, tile)
        piece = None
        for k in range(0, cols - 1, 2):
            few = range(k, min(k + 2, cols - 1))
            product = times_transposed(
                jnp.concatenate([left[i] for i in few], axis=1),
                jnp.concatenate([weight_refs[i][features, :] for i in few], axis=1),
            )
            piece = product if piece is None else piece + product
        sum_ref[:, features] = piece
    slot, count = slot_ref[0], held_ref.shape[0]
    slots = global_ref.shape[0] // count
    for load, source_ref, out_ref in zip(loads, (global_ref, moment_ref), (held_ref, prior_ref)):
        load.wait()
        picked = source_ref[pl.ds(0, count, stride=slots), :]
        for i in range(1, slots):
            picked = jnp.where(slot == i, source_ref[pl.ds(i, count, stride=slots), :], picked)
        out_ref[...] = picked
    store.wait()


def arrived(blocks, messages, sums, own, weights, cols, global_params, outer_moment, group_slot):
    rows, per_row = len(messages) + 1, len(blocks)
    size, width = blocks[0].shape
    depth = weights[0].shape[0]
    held = jax.ShapeDtypeStruct((global_params.shape[1] // LANES, LANES), jnp.float32)
    return pl.pallas_call(
        functools.partial(arrived_kernel, rows, cols, min(512, depth)),
        out_shape=[
            jax.ShapeDtypeStruct((size, depth), jnp.float32),
            jax.ShapeDtypeStruct((size, width), jnp.bfloat16),
            held,
            held,
            jax.ShapeDtypeStruct(own.shape, jnp.bfloat16),
        ],
        in_specs=[WHOLE] * (per_row + 2 * rows - 1 + cols - 1) + [pl.BlockSpec(memory_space=pltpu.SMEM), HBM, HBM],
        out_specs=[WHOLE] * 4 + [HBM],
        scratch_shapes=[
            pltpu.VMEM((cols, size, width), jnp.bfloat16),
            pltpu.VMEM(own.shape, jnp.bfloat16),
            pltpu.VMEM((global_params.size // LANES, LANES), jnp.float32),
            pltpu.VMEM((global_params.size // LANES, LANES), jnp.float32),
            pltpu.SemaphoreType.DMA,
            pltpu.SemaphoreType.DMA((2,)),
        ],
        compiler_params=params(24),
        cost_estimate=pl.CostEstimate(
            flops=2 * size * depth * width * (cols - 1), bytes_accessed=4 * size * depth, transcendentals=0
        ),
        name="arrived",
    )(
        *blocks, *messages, *sums, own, *weights, group_slot, in_hbm(interleaved(global_params)), in_hbm(interleaved(outer_moment))
    )


def finish_kernel(tile, count, sum_ref, block_ref, *refs):
    weight_refs = refs[:count]
    out_hbm, out_ref, sems = refs[count:]
    col = lax.axis_index("col")
    outside = (col == 0) | (col == lax.axis_size("col") - 1)
    stores = []
    for i, start in enumerate(range(0, sum_ref.shape[1], tile)):
        features = pl.ds(start, tile)
        weight = weight_refs[0][features, :]
        if count > 1:
            weight = jnp.where(outside, weight, weight_refs[1][features, :])
        piece = times_transposed(block_ref[...], weight)
        out_ref[:, features] = (sum_ref[:, features] + piece).astype(jnp.bfloat16)
        stores.append(pltpu.make_async_copy(out_ref.at[:, features], out_hbm.at[:, features], sems.at[i]))
        stores[-1].start()
    for store in stores:
        store.wait()


def finish(total, block, weights):
    size, depth = total.shape
    tile = min(512, depth)
    return pl.pallas_call(
        functools.partial(finish_kernel, tile, len(weights)),
        out_shape=jax.ShapeDtypeStruct((size, depth), jnp.bfloat16),
        in_specs=[WHOLE] * (2 + len(weights)),
        out_specs=HBM,
        scratch_shapes=[pltpu.VMEM((size, depth), jnp.bfloat16), pltpu.SemaphoreType.DMA((depth // tile,))],
        compiler_params=params(16),
        cost_estimate=pl.CostEstimate(
            flops=2 * size * depth * block.shape[1], bytes_accessed=6 * size * depth, transcendentals=0
        ),
        name="finish",
    )(total, block, *weights)


def merge_kernel(replicas, sum_ref, other_ref, held_ref, prior_ref, new_global_hbm, new_outer_hbm, *scratch):
    new_global_ref, new_outer_ref, sems = scratch
    average = (sum_ref[...].astype(jnp.float32) + other_ref[...].astype(jnp.float32)) / replicas
    new_outer = NESTEROV * prior_ref[...] + average
    new_outer_ref[...] = new_outer
    outer_store = pltpu.make_async_copy(new_outer_ref, new_outer_hbm, sems.at[0])
    outer_store.start()
    new_global_ref[...] = held_ref[...] - OUTER_RATE * (average + NESTEROV * new_outer)
    global_store = pltpu.make_async_copy(new_global_ref, new_global_hbm, sems.at[1])
    global_store.start()
    outer_store.wait()
    global_store.wait()


def interleaved(x):
    slots, size = x.shape
    return x.reshape(slots, size // LANES, LANES).transpose(1, 0, 2).reshape(slots * size // LANES, LANES)


def outer_sums(low, axis, early):
    n = lax.axis_size(axis)
    if not is_power_of_two(n):
        return lax.psum(low, axis), jnp.zeros_like(low)
    bit = 1
    while True:
        other = lax.ppermute(low, axis, swap_pairs(n, bit))
        bit *= 2
        if bit >= n:
            return low, other
        other, _ = after(other, early)
        low = (low.astype(jnp.float32) + other.astype(jnp.float32)).astype(jnp.bfloat16)


def merge(low, other, held, prior, replicas):
    shape = jax.ShapeDtypeStruct(low.shape, jnp.float32)
    new_global, new_outer = pl.pallas_call(
        functools.partial(merge_kernel, replicas),
        out_shape=[shape, shape],
        in_specs=[WHOLE] * 4,
        out_specs=[HBM] * 2,
        scratch_shapes=[pltpu.VMEM(low.shape, jnp.float32)] * 2 + [pltpu.SemaphoreType.DMA((2,))],
        compiler_params=params(16),
        cost_estimate=pl.CostEstimate(flops=8 * low.size, bytes_accessed=8 * low.size, transcendentals=0),
        name="merge",
    )(low, other, held, prior)
    return new_global.reshape(-1), new_outer.reshape(-1)


def on_device(
    tokens,
    cotangent,
    weight,
    first_moment,
    second_moment,
    outer_delta,
    global_params,
    outer_moment,
    group_slot,
):
    rows, cols = lax.axis_size("row"), lax.axis_size("col")
    replicas = lax.axis_size("rep")
    per_row = cols // rows
    cots = shifted(cotangent, "row")
    low_weight = rounded(weight[0])
    low, chunks = prepare(cotangent, outer_delta.reshape(-1, LANES), per_row)
    received = [lax.ppermute(chunks[k], ("row", "col"), chunk_pairs(rows, cols, per_row, k)) for k in range(per_row)]
    (new_weight, new_first, new_second), own, sends = inner(
        tokens, weight[0], first_moment[0], second_moment[0], cots, low_weight
    )
    weights, last = gather_blocks(low_weight, "col", sends)
    low, other = outer_sums(low, "rep", (sends, weights[1:]))
    received, _ = after(received, weights[1])
    sums = [lax.ppermute(m, "row", shift_pairs(rows, k + 1)) for k, m in enumerate(sends)]
    messages = [lax.ppermute(pack(received), "row", shift_pairs(rows, k)) for k in range(1, rows)]
    total, block, held, prior, keys_values = arrived(
        received, messages, sums, own, weights, cols, global_params, outer_moment, group_slot
    )
    new_global, new_outer = merge(low, other, held, prior, replicas)
    last, _ = after(last, (new_outer, total))
    input_grad = finish(total, block, last)
    return (keys_values, input_grad, new_weight[None], new_first[None], new_second[None], new_global, new_outer)


def solution(mesh):
    in_specs = (
        P("rep", "row"),
        P(("rep", "row"), "col"),
        P("rep", "row", "col"),
        P("rep", "row", "col"),
        P("rep", "row", "col"),
        P("rep", ("row", "col")),
        P(None, ("row", "col")),
        P(None, ("row", "col")),
        P(),
    )
    out_specs = (
        P(("rep", "row"), "col"),
        P(("rep", "col"), "row"),
        P("rep", "row", "col"),
        P("rep", "row", "col"),
        P("rep", "row", "col"),
        P(("row", "col")),
        P(("row", "col")),
    )
    return jax.shard_map(
        on_device, mesh=mesh, in_specs=in_specs, out_specs=out_specs, check_vma=False
    )
```
